32 devices in a mesh: grp: 2 (over x), site: 16 (over z, y, core).
Axes of the slice: x: 2, y: 2, z: 4, core: 2. Of those that a mesh axis runs over, the one named last changes fastest.
Arguments:
- vectors: float32 [4, 3, 16, 288, 256], P('grp', None, 'site'), parts along dimension 0, may hold values from -6 to 6
- links: float32 [6, 2, 3, 3, 16, 288], P('grp', None, None, None, 'site'), parts along dimension 0, may hold values from -1 to 1, as said below
- momenta: int32 [4, 3], replicated, may hold values from -2 to 2
- directions: int32 [256], replicated, may hold values from 0 to 2
Outputs:
- meson: float32 [256, 8, 2, 256], P('site', 'grp'), parts along dimension 1
The draws below stay inside these ranges and needn't reach their ends.
There are 2 independent parts, one for each index of `grp`. The reference program is written for one: setup_inputs(seed, part) draws one part's arguments, and reference() takes and returns one part's arrays. A program takes and returns all parts, laid end to end along the dimension named above; an argument that names none is the same for every part. Nothing has to cross between parts.
Inputs may be any that keep to these rules, and one draw needn't show every extreme that they name: Each links[k, :, :, :, t, s] holds the real and imaginary parts of a unitary 3 x 3 matrix.
All inputs are finite; a program needn't handle non-finite values.
Results may differ from the reference program's by a relative error of at most 0.0001.
Values sent between devices are 32-bit elements; how exact they have to be, the bound alone decides.
A program may use at most 128 MiB of HBM per device.

```python
import math
import jax
import jax.numpy as jnp
from jax import lax

NEV = 256
NMOM = 4
TLX = 12
TLY = 12
LZ = 2
NTX = 4
LX = 48
LY = 48
N_SITE = 16


def draw_links(key, part):
    shape = (3, 2, 3, 3, NTX * NTX, LZ * TLX * TLY)
    raw = jax.random.normal(key, shape, jnp.float32)
    columns = []
    for colour in range(3):
        v_real = raw[:, 0, :, colour]
        v_imag = raw[:, 1, :, colour]
        for q_real, q_imag in columns:
            p_real = jnp.sum(q_real * v_real + q_imag * v_imag, axis=1, keepdims=True)
            p_imag = jnp.sum(q_real * v_imag - q_imag * v_real, axis=1, keepdims=True)
            v_real = v_real - (p_real * q_real - p_imag * q_imag)
            v_imag = v_imag - (p_real * q_imag + p_imag * q_real)
        length = jnp.sqrt(jnp.sum(v_real * v_real + v_imag * v_imag, axis=1, keepdims=True))
        length = jnp.maximum(length, 0.001)
        columns.append((v_real / length, v_imag / length))
    real_part = jnp.stack([c[0] for c in columns], axis=2)
    imag_part = jnp.stack([c[1] for c in columns], axis=2)
    return jnp.stack([real_part, imag_part], axis=1).astype(jnp.float32)


def plant(drawn, stream_key, least, largest):
    shape = drawn.shape
    index_at = [jax.random.randint(jax.random.fold_in(stream_key, axis), (), 0, shape[axis]) for axis in range(len(shape))]
    drawn = drawn.at[tuple(index_at)].set(least)
    longest = shape.index(max(shape))
    index_at[longest] = (index_at[longest] + 1) % shape[longest]
    return drawn.at[tuple(index_at)].set(largest)


def block_levels(own_key, dims, pieces, smallest, top_value):
    factor_of, own = 1.0, jax.random.fold_in(own_key, 6)
    for dim, parts in pieces:
        heights = jnp.exp(jax.random.uniform(jax.random.fold_in(own, dim), (parts,), jnp.float32, smallest / len(pieces), top_value / len(pieces)))
        factor_of = factor_of * jnp.repeat(heights, dims[dim] // parts).reshape([-1 if axis == dim else 1 for axis in range(len(dims))])
    return factor_of


def bell_draw(own_key, extent, scale, most, pieces=(), kind=jnp.bfloat16):
    result = jax.random.normal(own_key, extent, jnp.float32) * scale
    if len(pieces) > 0:
        result = block_levels(own_key, extent, pieces, -0.22, 0.18) * result
    return jnp.clip(result, min=-most, max=most).astype(kind)


def setup_inputs(seed: int = 0, part: int = 0) -> dict:
    key_of = jax.random.split(jax.random.key(seed), 5)
    own_keys = jax.random.split(jax.random.fold_in(key_of[4], part), 5)
    vectors = bell_draw(own_keys[0], (2, 3, N_SITE, LZ * TLX * TLY, NEV), 1.0, 6.0, ((2, 16),), jnp.float32)
    links = draw_links(jax.random.fold_in(jax.random.fold_in(key_of[4], part), 71), part)
    momenta = plant(jax.random.randint(key_of[2], (NMOM, 3), -2, 3), jax.random.fold_in(key_of[2], 1), -2, 2).astype(jnp.int32)
    directions = plant(jax.random.randint(key_of[3], (NEV,), 0, 3), jax.random.fold_in(key_of[3], 1), 0, 2).astype(jnp.int32)
    return {"vectors": vectors, "links": links, "momenta": momenta, "directions": directions}


kappa = 0.08

def to_lattice(arr, tiles, planes, tile_x, tile_y, trailing):
    count = arr.ndim - 2 - trailing
    lead = arr.shape[:count]
    trail = arr.shape[count + 2:]
    grid = arr.reshape(lead + (tiles, tiles, planes, tile_x, tile_y) + trail)
    order = tuple(range(count)) + (count + 2, count, count + 3, count + 1, count + 4)
    order = order + tuple(range(count + 5, count + 5 + trailing))
    grid = jnp.transpose(grid, order)
    return grid.reshape(lead + (planes, tiles * tile_x, tiles * tile_y) + trail)

def mat_apply(link_k, field):
    real_part = 0.0
    imag_part = 0.0
    for colour in range(3):
        u_real = link_k[0, :, colour][..., None]
        u_imag = link_k[1, :, colour][..., None]
        f_real = field[0, colour][None]
        f_imag = field[1, colour][None]
        real_part = real_part + u_real * f_real - u_imag * f_imag
        imag_part = imag_part + u_real * f_imag + u_imag * f_real
    return jnp.stack([real_part, imag_part])

def adj_apply(link_k, field):
    real_part = 0.0
    imag_part = 0.0
    for colour in range(3):
        u_real = link_k[0, colour][..., None]
        u_imag = link_k[1, colour][..., None]
        f_real = field[0, colour][None]
        f_imag = field[1, colour][None]
        real_part = real_part + u_real * f_real + u_imag * f_imag
        imag_part = imag_part + u_real * f_imag - u_imag * f_real
    return jnp.stack([real_part, imag_part])

def next_y(field):
    rolled = jnp.roll(field, -1, -2)
    edge = jnp.roll(field[..., 0, :], -TLX, -2)
    return jnp.concatenate([rolled[..., :-1, :], edge[..., None, :]], axis=-2)

def prev_y(field):
    rolled = jnp.roll(field, 1, -2)
    edge = jnp.roll(field[..., -1, :], TLX, -2)
    return jnp.concatenate([edge[..., None, :], rolled[..., 1:, :]], axis=-2)

def hop_terms(field, links, sign):
    terms = []
    forward = mat_apply(links[0], jnp.roll(field, -1, -3))
    backward = jnp.roll(adj_apply(links[0], field), 1, -3)
    terms.append(forward + sign * backward)
    forward = mat_apply(links[1], next_y(field))
    backward = prev_y(adj_apply(links[1], field))
    terms.append(forward + sign * backward)
    forward = mat_apply(links[2], jnp.roll(field, -1, -4))
    backward = jnp.roll(adj_apply(links[2], field), 1, -4)
    terms.append(forward + sign * backward)
    return terms

def smear_step(field, links):
    terms = hop_terms(field, links, 1.0)
    return field + kappa * (terms[0] + terms[1] + terms[2] - 6.0 * field)

def displace(field, links, masks):
    terms = hop_terms(field, links, -1.0)
    total = 0.0
    for which in range(3):
        total = total + masks[which][None, None, None, None, None, :] * terms[which]
    return total

def meson_fields(left_field, shifted, momenta, xs, ys, zs, lx, ly, planes, scale):
    nev = left_field.shape[-1]
    flat_v = left_field.reshape((2, 3, -1, nev))
    flat_s = shifted.reshape((2, 3, -1, nev))
    blocks = []
    for moment in range(momenta.shape[0]):
        frac = (momenta[moment, 0] * xs % lx).astype(jnp.float32) / lx
        frac = frac + (momenta[moment, 1] * ys % ly).astype(jnp.float32) / ly
        frac = frac + (momenta[moment, 2] * zs % planes).astype(jnp.float32) / planes
        theta = (2.0 * math.pi * frac).reshape(-1)
        cosine = jnp.cos(theta)[:, None]
        sine = jnp.sin(theta)[:, None]
        a_real = cosine * flat_v[0] - sine * flat_v[1]
        a_imag = -(sine * flat_v[0] + cosine * flat_v[1])
        left = jnp.stack([a_real, a_imag])
        prods = jnp.einsum('acsn,bcsm->anbm', left, flat_s, precision=lax.Precision.HIGHEST)
        re_block = prods[0, :, 0] - prods[1, :, 1]
        im_block = prods[0, :, 1] + prods[1, :, 0]
        blocks.append(jnp.stack([re_block, im_block], axis=1))
    return jnp.stack(blocks, axis=1) * scale

def reference(vectors, links, momenta, directions):
    masks = (directions[None, :] == jnp.arange(3, dtype=jnp.int32)[:, None]).astype(jnp.float32)
    field = to_lattice(vectors, NTX, LZ, TLX, TLY, 1)
    lattice_links = to_lattice(links, NTX, LZ, TLX, TLY, 0)
    once = smear_step(field, lattice_links)
    twice = smear_step(once, lattice_links)
    shifted = displace(twice, lattice_links, masks)
    zs = jnp.arange(LZ, dtype=jnp.int32)[:, None, None]
    xs = jnp.arange(LX, dtype=jnp.int32)[None, :, None]
    ys = jnp.arange(LY, dtype=jnp.int32)[None, None, :]
    scale = 1.0 / math.sqrt(3.0 * LX * LY * LZ)
    return meson_fields(field, shifted, momenta, xs, ys, zs, LX, LY, LZ, scale)
```

```python
import functools
import math

import jax
import jax.numpy as jnp
from jax import lax
from jax.experimental import pallas as pl
from jax.experimental.pallas import tpu as pltpu
from jax.sharding import PartitionSpec as P

TLX = 12
TLY = 12
LZ = 2
YP = 16
KAPPA = 0.08
SIDE = TLX * LZ
F32 = jnp.float32
BF16 = jnp.bfloat16
MAIN = LZ * TLX * YP
HALO = 2 * LZ * YP
KHALF = 3 * MAIN + 4 * HALO


def mat(u, f):
    out = []
    for a in range(3):
        re = im = None
        for b in range(3):
            ur, ui = u[a][b]
            fr, fi = f[b]
            tr = ur * fr - ui * fi
            ti = ur * fi + ui * fr
            re = tr if re is None else re + tr
            im = ti if im is None else im + ti
        out.append((re, im))
    return out


def adj(u, f):
    out = []
    for a in range(3):
        re = im = None
        for b in range(3):
            ur, ui = u[b][a]
            fr, fi = f[b]
            tr = ur * fr + ui * fi
            ti = ur * fi - ui * fr
            re = tr if re is None else re + tr
            im = ti if im is None else im + ti
        out.append((re, im))
    return out


def kernel(n, tiles, nmom, v_ref, lk_ref, lkx_ref, lky_ref, cs_ref, dir_ref, out_ref,
           fv, fo, ft, links, send_buf, recv_buf, lh, ll, rh, rl, part, got,
           send_sem, recv_sem, rs_send, rs_recv):
    nev = v_ref.shape[-1]
    rows = nev // n
    stages = n.bit_length() - 1
    me = lax.axis_index("site")
    above_x = lax.rem(me + tiles, n)
    below_x = lax.rem(me + n - tiles, n)
    above_y = lax.rem(me + 1, n)
    below_y = lax.rem(me + n - 1, n)
    partners = []
    bits = []
    for s in range(stages):
        bit = (me // (1 << s)) % 2
        bits.append(bit)
        partners.append(me + (1 - 2 * bit) * (1 << s))

    barrier = pltpu.get_barrier_semaphore()
    greeted = [above_x, below_x, above_y, below_y] + partners
    for other in greeted:
        pl.semaphore_signal(barrier, inc=1, device_id={"site": other},
                            device_id_type=pl.DeviceIdType.MESH)

    zero_rows = jnp.zeros((YP, nev), F32)

    def fill(x, carry):
        for c in range(6):
            for z in range(LZ):
                fv[c, z, x] = zero_rows
                ft[c, z, x] = zero_rows
                fo[c, z, x] = zero_rows
        return carry

    lax.fori_loop(0, TLX + 2, fill, 0)
    for c in range(6):
        for z in range(LZ):
            for x in range(TLX):
                start = (z * TLX + x) * TLY
                fv[c, z, x + 1, 0:TLY, :] = v_ref[c, start:start + TLY, :]

    def compact(ref):
        def one(k):
            return jnp.broadcast_to(ref[:, k:k + 1], (SIDE, nev))
        return [[(one(3 * a + b), one(9 + 3 * a + b)) for b in range(3)] for a in range(3)]

    def halo_copies(rnd):
        targets = (below_x, above_x, below_y, above_y)
        return [
            pltpu.make_async_remote_copy(
                src_ref=send_buf.at[rnd, i], dst_ref=recv_buf.at[rnd, i],
                send_sem=send_sem.at[rnd, i], recv_sem=recv_sem.at[rnd, i],
                device_id={"site": targets[i]}, device_id_type=pl.DeviceIdType.MESH)
            for i in range(4)
        ]

    def pack_x(src, rnd, slot, layer):
        for c in range(6):
            for z in range(LZ):
                send_buf[rnd, slot, c, z * TLX:(z + 1) * TLX, :] = src[c, z, layer, 0:TLY, :]

    def pack_y(src, rnd, slot, row):
        for c in range(6):
            for z in range(LZ):
                send_buf[rnd, slot, c, z * TLX:(z + 1) * TLX, :] = src[c, z, 1:TLX + 1, row, :]

    def turn(rnd, slot, ref):
        u = compact(ref)
        f = [(send_buf[rnd, slot, b], send_buf[rnd, slot, 3 + b]) for b in range(3)]
        g = adj(u, f)
        for a in range(3):
            send_buf[rnd, slot, a] = g[a][0]
            send_buf[rnd, slot, 3 + a] = g[a][1]

    def pack_all(src, rnd):
        pack_x(src, rnd, 0, 1)
        pack_x(src, rnd, 1, TLX)
        turn(rnd, 1, lkx_ref)
        pack_y(src, rnd, 2, 0)
        pack_y(src, rnd, 3, TLY - 1)
        turn(rnd, 3, lky_ref)

    def unpack_all(dst, rnd):
        for c in range(6):
            for z in range(LZ):
                part_rows = slice(z * TLX, (z + 1) * TLX)
                dst[c, z, TLX + 1, 0:TLY, :] = recv_buf[rnd, 0, c, part_rows, :]
                dst[c, z, 0, 0:TLY, :] = recv_buf[rnd, 1, c, part_rows, :]
                dst[c, z, 1:TLX + 1, TLY, :] = recv_buf[rnd, 2, c, part_rows, :]
                dst[c, z, 1:TLX + 1, YP - 1, :] = recv_buf[rnd, 3, c, part_rows, :]

    pack_all(fv, 0)
    pl.semaphore_wait(barrier, len(greeted))
    first = halo_copies(0)
    for copy in first:
        copy.start()

    def spread(r, carry):
        at = pl.multiple_of(r * YP, YP)
        block = lk_ref[pl.ds(at, YP), :]
        for k in range(54):
            links[k, pl.ds(at, YP), :] = jnp.broadcast_to(block[:, k:k + 1], (YP, 128))
        return carry

    lax.fori_loop(0, LZ * (TLX + 1), spread, 0)

    def link(k, z, layer):
        at = pl.multiple_of((z * (TLX + 1) + layer) * YP, YP)
        def one(i):
            return links[18 * k + i, pl.ds(at, YP), :]
        return [[(one(3 * a + b), one(9 + 3 * a + b)) for b in range(3)] for a in range(3)]

    def load(src, z, layer, lanes):
        return [(src[b, z, layer, :, lanes], src[3 + b, z, layer, :, lanes]) for b in range(3)]

    def roll(f, shift):
        return [(pltpu.roll(r, shift, 0), pltpu.roll(i, shift, 0)) for r, i in f]

    def hops(src, z, x, lanes, k):
        f = load(src, z, x + 1, lanes)
        if k == 0:
            return (mat(link(0, z, x + 1), load(src, z, x + 2, lanes)),
                    adj(link(0, z, x), load(src, z, x, lanes)))
        if k == 1:
            u = link(1, z, x + 1)
            return mat(u, roll(f, YP - 1)), roll(adj(u, f), 1)
        other = load(src, 1 - z, x + 1, lanes)
        return mat(link(2, z, x + 1), other), adj(link(2, 1 - z, x + 1), other)

    real_row = lax.broadcasted_iota(jnp.int32, (YP, 128), 0) < TLY

    def smear(src, dst):
        def body(x, carry):
            for z in range(LZ):
                for half in range(nev // 128):
                    lanes = slice(half * 128, (half + 1) * 128)
                    total = None
                    for k in range(3):
                        fwd, bwd = hops(src, z, x, lanes, k)
                        term = [(a[0] + b[0], a[1] + b[1]) for a, b in zip(fwd, bwd)]
                        total = term if total is None else [
                            (a[0] + b[0], a[1] + b[1]) for a, b in zip(total, term)]
                    f = load(src, z, x + 1, lanes)
                    for a in range(3):
                        for p in range(2):
                            new = f[a][p] + KAPPA * (total[a][p] - 6.0 * f[a][p])
                            dst[3 * p + a, z, x + 1, :, lanes] = jnp.where(real_row, new, 0.0)
            return carry
        lax.fori_loop(0, TLX, body, 0)

    for copy in first:
        copy.wait()
    unpack_all(fv, 0)
    smear(fv, fo)
    pack_all(fo, 1)
    second = halo_copies(1)
    for copy in second:
        copy.start()

    pieces = []
    for c in range(3):
        pieces += [(c, z, x + 1) for z in range(LZ) for x in range(TLX)]
    for c in range(3):
        pieces += [(c, z, layer) for layer in (TLX + 1, 0) for z in range(LZ)]
    pieces += [None] * (2 * LZ)
    per = 128 // YP
    for chunk in range(KHALF // 128):
        mine = pieces[chunk * per:(chunk + 1) * per]
        vr = jnp.concatenate([zero_rows if q is None else fv[q[0], q[1], q[2]] for q in mine], 0)
        vi = jnp.concatenate([zero_rows if q is None else fv[3 + q[0], q[1], q[2]] for q in mine], 0)
        vr = vr.T
        vi = vi.T
        lanes = slice(chunk * 128, (chunk + 1) * 128)
        lanes_i = slice(KHALF + chunk * 128, KHALF + (chunk + 1) * 128)
        for m in range(nmom):
            co = cs_ref[2 * m:2 * m + 1, lanes]
            si = cs_ref[2 * m + 1:2 * m + 2, lanes]
            ar = co * vr - si * vi
            ai = -(si * vr + co * vi)
            for a, where_to in ((ar, lanes), (ai, lanes_i)):
                hi = a.astype(BF16)
                lh[m * nev:(m + 1) * nev, where_to] = hi
                ll[m * nev:(m + 1) * nev, where_to] = (a - hi.astype(F32)).astype(BF16)

    for copy in second:
        copy.wait()
    unpack_all(fo, 1)
    smear(fo, ft)

    def put(row, col, value):
        hi = value.astype(BF16)
        rh[pl.ds(row, YP), col] = hi
        rl[pl.ds(row, YP), col] = (value - hi.astype(F32)).astype(BF16)

    def put_complex(row, half, s):
        left = slice(half * 128, (half + 1) * 128)
        right = slice(nev + half * 128, nev + (half + 1) * 128)
        put(row, left, s[0])
        put(row, right, s[1])
        put(row + KHALF, left, -s[1])
        put(row + KHALF, right, s[0])

    def displace(x, carry):
        for z in range(LZ):
            for half in range(nev // 128):
                lanes = slice(half * 128, (half + 1) * 128)
                which = dir_ref[0:1, lanes]
                diffs = []
                for k in range(3):
                    fwd, bwd = hops(ft, z, x, lanes, k)
                    diffs.append([(a[0] - b[0], a[1] - b[1]) for a, b in zip(fwd, bwd)])
                for c in range(3):
                    s = tuple(jnp.where(which == 0, diffs[0][c][p],
                                        jnp.where(which == 1, diffs[1][c][p], diffs[2][c][p]))
                              for p in range(2))
                    put_complex(pl.multiple_of(c * MAIN + (z * TLX + x) * YP, YP), half, s)
        return carry

    lax.fori_loop(0, TLX, displace, 0)
    for z in range(LZ):
        for half in range(nev // 128):
            lanes = slice(half * 128, (half + 1) * 128)
            on_x = dir_ref[0:1, lanes] == 0
            high = adj(link(0, z, TLX), load(ft, z, TLX, lanes))
            low = load(ft, z, 1, lanes)
            for c in range(3):
                base = 3 * MAIN + c * HALO + z * YP
                put_complex(base, half, tuple(jnp.where(on_x, -high[c][p], 0.0) for p in range(2)))
                put_complex(base + LZ * YP, half,
                            tuple(jnp.where(on_x, low[c][p], 0.0) for p in range(2)))
    zero_tail = jnp.zeros((HALO, 2 * nev), BF16)
    for base in (KHALF - HALO, 2 * KHALF - HALO):
        rh[base:base + HALO, :] = zero_tail
        rl[base:base + HALO, :] = zero_tail

    def reversed_bits(o):
        return sum(((o >> s) & 1) << (stages - 1 - s) for s in range(stages))

    got_at = [0]
    for s in range(stages):
        got_at.append(got_at[-1] + (n >> (s + 1)))
    bases = [0]
    for s in range(stages):
        bases.append(bases[-1] + bits[s] * (n >> (s + 1)))
    copies = {}

    def launch(m, s):
        size = n >> (s + 1)
        copies[m, s] = pltpu.make_async_remote_copy(
            src_ref=part.at[m, pl.ds(bases[s] + (1 - bits[s]) * size, size)],
            dst_ref=got.at[m, pl.ds(got_at[s], size)],
            send_sem=rs_send.at[m, s], recv_sem=rs_recv.at[m, s],
            device_id={"site": partners[s]}, device_id_type=pl.DeviceIdType.MESH)
        copies[m, s].start()

    for tick in range(nmom + stages):
        if tick < nmom:
            m = tick
            take = slice(m * nev, (m + 1) * nev)
            prod = jnp.dot(lh[take, :], rh[...], preferred_element_type=F32)
            prod = prod + jnp.dot(lh[take, :], rl[...], preferred_element_type=F32)
            prod = prod + jnp.dot(ll[take, :], rh[...], preferred_element_type=F32)
            for o in range(n):
                part[m, reversed_bits(o)] = prod[o * rows:(o + 1) * rows, :]
            launch(m, 0)
        for s in range(stages - 1, -1, -1):
            m = tick - 1 - s
            if 0 <= m < nmom:
                copies[m, s].wait()
                size = n >> (s + 1)
                keep = pl.ds(bases[s + 1], size)
                summed = part[m, keep] + got[m, got_at[s]:got_at[s] + size]
                if s + 1 < stages:
                    part[m, keep] = summed
                    launch(m, s + 1)
                else:
                    out_ref[m] = summed[0]


def on_device(vectors, links, momenta, directions):
    n = lax.axis_size("site")
    tiles = math.isqrt(n)
    position = lax.axis_index("site")
    tile_row = position // tiles
    tile_col = position % tiles
    nev = vectors.shape[-1]
    nmom = momenta.shape[0]
    rows = nev // n
    stages = n.bit_length() - 1
    lx = TLX * tiles
    ly = TLY * tiles
    field = vectors.reshape((6, LZ * TLX * TLY, nev))
    local = links.reshape((3, 18, LZ, TLX, TLY))
    unit = jnp.concatenate([jnp.eye(3, dtype=F32).reshape(9), jnp.zeros(9, F32)])
    lkx = jnp.pad(local[0, :, :, TLX - 1].reshape(18, SIDE).T, ((0, 0), (0, 110)))
    lky = jnp.pad(local[1, :, :, :, TLY - 1].reshape(18, SIDE).T, ((0, 0), (0, 110)))
    flat = local.reshape(54, LZ, TLX, TLY).transpose(1, 2, 3, 0)
    zeros18 = jnp.zeros(18, F32)
    edge_y = jnp.concatenate([zeros18, unit, zeros18])
    edge_x = jnp.concatenate([unit, zeros18, zeros18])
    flat = jnp.concatenate([
        flat, jnp.zeros((LZ, TLX, YP - TLY - 1, 54), F32),
        jnp.broadcast_to(edge_y, (LZ, TLX, 1, 54))], axis=2)
    flat = jnp.concatenate([jnp.broadcast_to(edge_x, (LZ, 1, YP, 54)), flat], axis=1)
    lk = jnp.pad(flat.reshape(LZ * (TLX + 1) * YP, 54), ((0, 0), (0, 74)))

    ypos = jnp.arange(YP, dtype=jnp.int32)
    ypos = jnp.where(ypos == YP - 1, -1, ypos)
    gy = (tile_col * TLY + ypos)[None, None, :]
    xs = jnp.concatenate([jnp.arange(TLX), jnp.array([TLX, -1])]).astype(jnp.int32)
    gx = (tile_row * TLX + xs)[None, :, None]
    gx = gx + TLX * (gy >= ly).astype(jnp.int32) - TLX * (gy < 0).astype(jnp.int32)
    gx = jnp.mod(gx, lx)
    gy = jnp.mod(gy, ly)
    gz = jnp.arange(LZ, dtype=jnp.int32)[:, None, None]
    mom = momenta[:, :, None, None, None]
    frac = (mom[:, 0] * gx % lx).astype(F32) / lx
    frac = frac + (mom[:, 1] * gy % ly).astype(F32) / ly
    frac = frac + (mom[:, 2] * gz % LZ).astype(F32) / LZ
    theta = 2.0 * math.pi * frac
    scale = 1.0 / math.sqrt(3.0 * lx * ly * LZ)
    cs = jnp.stack([jnp.cos(theta), jnp.sin(theta)], axis=1) * scale
    main = cs[:, :, :, :TLX].reshape(2 * nmom, MAIN)
    halo = cs[:, :, :, TLX:].transpose(0, 1, 3, 2, 4).reshape(2 * nmom, HALO)
    cs = jnp.concatenate([main] * 3 + [halo] * 4, axis=1)

    vmem = pl.BlockSpec(memory_space=pltpu.VMEM)
    ext = pltpu.VMEM((6, LZ, TLX + 2, YP, nev), F32)
    out = pl.pallas_call(
        functools.partial(kernel, n, tiles, nmom),
        out_shape=jax.ShapeDtypeStruct((nmom, rows, 2 * nev), F32),
        in_specs=[vmem] * 6,
        out_specs=vmem,
        scratch_shapes=[
            ext, ext, ext,
            pltpu.VMEM((54, LZ * (TLX + 1) * YP, 128), F32),
            pltpu.VMEM((2, 4, 6, SIDE, nev), F32),
            pltpu.VMEM((2, 4, 6, SIDE, nev), F32),
            pltpu.VMEM((nmom * nev, 2 * KHALF), BF16),
            pltpu.VMEM((nmom * nev, 2 * KHALF), BF16),
            pltpu.VMEM((2 * KHALF, 2 * nev), BF16),
            pltpu.VMEM((2 * KHALF, 2 * nev), BF16),
            pltpu.VMEM((nmom, n, rows, 2 * nev), F32),
            pltpu.VMEM((nmom, n, rows, 2 * nev), F32),
            pltpu.SemaphoreType.DMA((2, 4)),
            pltpu.SemaphoreType.DMA((2, 4)),
            pltpu.SemaphoreType.DMA((nmom, stages)),
            pltpu.SemaphoreType.DMA((nmom, stages)),
        ],
        compiler_params=pltpu.CompilerParams(
            collective_id=0, has_side_effects=True, vmem_limit_bytes=60 * 1024 * 1024),
    )(field, lk, lkx, lky, cs, directions.reshape(1, nev))
    return out.reshape(nmom, rows, 2, nev).transpose(1, 0, 2, 3)


def solution(mesh):
    placed = (
        P("grp", None, "site", None, None),
        P("grp", None, None, None, "site", None),
        P(),
        P(),
    )
    return jax.shard_map(
        on_device,
        mesh=mesh,
        in_specs=placed,
        out_specs=P("site", "grp", None, None),
        check_vma=False,
    )
```

```python
import functools
import math

import jax
import jax.numpy as jnp
import numpy as np
from jax import lax
from jax.experimental import pallas as pl
from jax.experimental.pallas import tpu as pltpu
from jax.sharding import PartitionSpec as P

TLX = 12
TLY = 12
LZ = 2
YP = 16
KAPPA = 0.08
SIDE = TLX * LZ
F32 = jnp.float32
BF16 = jnp.bfloat16
MAIN = LZ * TLX * YP
HALO = 2 * LZ * YP
KHALF = 3 * MAIN + 4 * HALO


def mat(u, f):
    out = []
    for a in range(3):
        re = im = None
        for b in range(3):
            ur, ui = u[a][b]
            fr, fi = f[b]
            tr = ur * fr - ui * fi
            ti = ur * fi + ui * fr
            re = tr if re is None else re + tr
            im = ti if im is None else im + ti
        out.append((re, im))
    return out


def adj(u, f):
    out = []
    for a in range(3):
        re = im = None
        for b in range(3):
            ur, ui = u[b][a]
            fr, fi = f[b]
            tr = ur * fr + ui * fi
            ti = ur * fi - ui * fr
            re = tr if re is None else re + tr
            im = ti if im is None else im + ti
        out.append((re, im))
    return out


def kernel(n, tiles, nmom, v_ref, lk_ref, pos_ref, mom_ref, dir_ref, out_ref,
           fv, fo, ft, links, lkw, lkt, lkp, lkx, lky, cs, send_buf, recv_buf, lh, ll, rh, rl,
           part, got, send_sem, recv_sem, rs_send, rs_recv):
    nev = v_ref.shape[-1]
    halves = nev // 128
    rows = nev // n
    stages = n.bit_length() - 1
    me = lax.axis_index("site")
    above_x = lax.rem(me + tiles, n)
    below_x = lax.rem(me + n - tiles, n)
    above_y = lax.rem(me + 1, n)
    below_y = lax.rem(me + n - 1, n)
    partners = []
    bits = []
    for s in range(stages):
        bit = (me // (1 << s)) % 2
        bits.append(bit)
        partners.append(me + (1 - 2 * bit) * (1 << s))

    barrier = pltpu.get_barrier_semaphore()
    greeted = [above_x, below_x, above_y, below_y] + partners
    for other in greeted:
        pl.semaphore_signal(barrier, inc=1, device_id={"site": other},
                            device_id_type=pl.DeviceIdType.MESH)

    def lanes_of(half):
        return slice(half * 128, (half + 1) * 128)

    lkw[...] = jnp.zeros_like(lkw)
    lkw[0:54, 0:SIDE * TLY] = lk_ref[...]
    lkt[...] = lkw[...].T
    lane = lax.broadcasted_iota(jnp.int32, (YP, 128), 1)
    row = lax.broadcasted_iota(jnp.int32, (YP, 128), 0)
    unit_x = jnp.where((lane == 0) | (lane == 4) | (lane == 8), 1.0, 0.0)
    unit_y = jnp.where(((lane == 18) | (lane == 22) | (lane == 26)) & (row == YP - 1), 1.0, 0.0)
    for z in range(LZ):
        lkp[z, 0] = unit_x
        for x in range(TLX):
            first_row = (z * TLX + x) * TLY
            lkp[z, x + 1] = unit_y
            lkp[z, x + 1, 0:TLY, :] = lkt[first_row:first_row + TLY, :]
        last = (z + 1) * TLX * TLY - TLY
        lkx[z * TLX:(z + 1) * TLX, :] = lkt[last:last + TLY, :]
    lky[...] = lkt[pl.ds(TLY - 1, SIDE, stride=TLY), :]

    def compact(ref, k):
        def one(i):
            return jnp.broadcast_to(ref[:, 18 * k + i:18 * k + i + 1], (SIDE, 128))
        return [[(one(3 * a + b), one(9 + 3 * a + b)) for b in range(3)] for a in range(3)]

    def halo_copies(rnd, half):
        targets = (below_x, above_x, below_y, above_y)
        return [
            pltpu.make_async_remote_copy(
                src_ref=send_buf.at[rnd, half, i], dst_ref=recv_buf.at[rnd, half, i],
                send_sem=send_sem.at[rnd, half, i], recv_sem=recv_sem.at[rnd, half, i],
                device_id={"site": targets[i]}, device_id_type=pl.DeviceIdType.MESH)
            for i in range(4)
        ]

    def turn(rnd, half, slot, ref, k):
        u = compact(ref, k)
        f = [(send_buf[rnd, half, slot, b], send_buf[rnd, half, slot, 3 + b]) for b in range(3)]
        g = adj(u, f)
        for a in range(3):
            send_buf[rnd, half, slot, a] = g[a][0]
            send_buf[rnd, half, slot, 3 + a] = g[a][1]

    def pack_given(half):
        lanes = lanes_of(half)
        for c in range(6):
            p, b = c // 3, c % 3
            for z in range(LZ):
                at = z * TLX * TLY
                last = at + TLX * TLY - TLY
                to = slice(z * TLX, (z + 1) * TLX)
                send_buf[0, half, 0, c, to, :] = v_ref[p, b, 0, at:at + TLY, lanes]
                send_buf[0, half, 1, c, to, :] = v_ref[p, b, 0, last:last + TLY, lanes]
                for x in range(TLX):
                    i = z * TLX + x
                    send_buf[0, half, 2, c, i:i + 1, :] = v_ref[p, b, 0, at + x * TLY:at + x * TLY + 1, lanes]
                    y = at + x * TLY + TLY - 1
                    send_buf[0, half, 3, c, i:i + 1, :] = v_ref[p, b, 0, y:y + 1, lanes]
        turn(0, half, 1, lkx, 0)
        turn(0, half, 3, lky, 1)

    def pack(src, rnd, half):
        lanes = lanes_of(half)
        for c in range(6):
            for z in range(LZ):
                to = slice(z * TLX, (z + 1) * TLX)
                send_buf[rnd, half, 0, c, to, :] = src[c, z, 1, 0:TLY, lanes]
                send_buf[rnd, half, 1, c, to, :] = src[c, z, TLX, 0:TLY, lanes]
                send_buf[rnd, half, 2, c, to, :] = src[c, z, 1:TLX + 1, 0, lanes]
                send_buf[rnd, half, 3, c, to, :] = src[c, z, 1:TLX + 1, TLY - 1, lanes]
        turn(rnd, half, 1, lkx, 0)
        turn(rnd, half, 3, lky, 1)

    def unpack(dst, rnd, half):
        lanes = lanes_of(half)
        for c in range(6):
            for z in range(LZ):
                at = slice(z * TLX, (z + 1) * TLX)
                dst[c, z, TLX + 1, 0:TLY, lanes] = recv_buf[rnd, half, 0, c, at, :]
                dst[c, z, 0, 0:TLY, lanes] = recv_buf[rnd, half, 1, c, at, :]
                dst[c, z, 1:TLX + 1, TLY, lanes] = recv_buf[rnd, half, 2, c, at, :]
                dst[c, z, 1:TLX + 1, YP - 1, lanes] = recv_buf[rnd, half, 3, c, at, :]

    flying = {}

    def send(rnd, half):
        flying[rnd, half] = halo_copies(rnd, half)
        for copy in flying[rnd, half]:
            copy.start()

    def receive(rnd, half):
        for copy in flying[rnd, half]:
            copy.wait()

    pack_given(0)
    pl.semaphore_wait(barrier, len(greeted))
    send(0, 0)
    for half in range(1, halves):
        pack_given(half)
        send(0, half)

    zero_pad = jnp.zeros((YP - TLY, nev), F32)
    zero_rows = jnp.zeros((YP, nev), F32)
    for c in range(6):
        for z in range(LZ):
            for layer in (0, TLX + 1):
                fv[c, z, layer, TLY:YP, :] = zero_pad
                ft[c, z, layer] = zero_rows
            for x in range(TLX):
                at = (z * TLX + x) * TLY
                fv[c, z, x + 1, 0:TLY, :] = v_ref[c // 3, c % 3, 0, at:at + TLY, :]
                fv[c, z, x + 1, TLY:YP, :] = zero_pad

    def spread(r, carry):
        at = pl.multiple_of(r * YP, YP)
        block = lkp[r // (TLX + 1), r % (TLX + 1)]
        for k in range(54):
            links[k, pl.ds(at, YP), :] = jnp.broadcast_to(block[:, k:k + 1], (YP, 128))
        return carry

    lax.fori_loop(0, LZ * (TLX + 1), spread, 0)

    lx = TLX * tiles
    ly = TLY * tiles
    gx = (me // tiles) * TLX + pos_ref[0:1, :]
    gy = (me % tiles) * TLY + pos_ref[1:2, :]
    gx = gx + jnp.where(gy >= ly, TLX, 0) - jnp.where(gy < 0, TLX, 0)
    gy = gy - jnp.where(gy >= ly, ly, 0) + jnp.where(gy < 0, ly, 0)
    gx = gx - jnp.where(gx >= lx, lx, 0) + jnp.where(gx < 0, lx, 0)
    mom = mom_ref[...].astype(F32)

    def turns(k, at, extent):
        f = mom[:, k:k + 1] * at.astype(F32) / extent
        return f - jnp.floor(f)

    theta = 2.0 * math.pi * (turns(0, gx, lx) + turns(1, gy, ly) + turns(2, pos_ref[2:3, :], LZ))
    scale = 1.0 / math.sqrt(3.0 * lx * ly * LZ)
    cs[0] = jnp.cos(theta) * scale
    cs[1] = jnp.sin(theta) * scale

    def link(k, z, layer):
        at = pl.multiple_of((z * (TLX + 1) + layer) * YP, YP)
        def one(i):
            return links[18 * k + i, pl.ds(at, YP), :]
        return [[(one(3 * a + b), one(9 + 3 * a + b)) for b in range(3)] for a in range(3)]

    def load(src, z, layer, lanes):
        return [(src[b, z, layer, :, lanes], src[3 + b, z, layer, :, lanes]) for b in range(3)]

    def roll(f, shift):
        return [(pltpu.roll(r, shift, 0), pltpu.roll(i, shift, 0)) for r, i in f]

    def hops(src, z, x, lanes, k):
        f = load(src, z, x + 1, lanes)
        if k == 0:
            return (mat(link(0, z, x + 1), load(src, z, x + 2, lanes)),
                    adj(link(0, z, x), load(src, z, x, lanes)))
        if k == 1:
            u = link(1, z, x + 1)
            return mat(u, roll(f, YP - 1)), roll(adj(u, f), 1)
        other = load(src, 1 - z, x + 1, lanes)
        return mat(link(2, z, x + 1), other), adj(link(2, 1 - z, x + 1), other)

    real_row = row < TLY

    def smear(src, dst, half):
        lanes = lanes_of(half)

        def body(x, carry):
            for z in range(LZ):
                total = None
                for k in range(3):
                    fwd, bwd = hops(src, z, x, lanes, k)
                    term = [(a[0] + b[0], a[1] + b[1]) for a, b in zip(fwd, bwd)]
                    total = term if total is None else [
                        (a[0] + b[0], a[1] + b[1]) for a, b in zip(total, term)]
                f = load(src, z, x + 1, lanes)
                for a in range(3):
                    for p in range(2):
                        new = f[a][p] + KAPPA * (total[a][p] - 6.0 * f[a][p])
                        dst[3 * p + a, z, x + 1, :, lanes] = jnp.where(real_row, new, 0.0)
            return carry

        lax.fori_loop(0, TLX, body, 0)

    for half in range(halves):
        receive(0, half)
        unpack(fv, 0, half)
        smear(fv, fo, half)
        pack(fo, 1, half)
        send(1, half)

    pieces = []
    for c in range(3):
        pieces += [(c, z, x + 1) for z in range(LZ) for x in range(TLX)]
    for c in range(3):
        pieces += [(c, z, layer) for layer in (TLX + 1, 0) for z in range(LZ)]
    pieces += [None] * (2 * LZ)
    per = 128 // YP
    for chunk in range(KHALF // 128):
        mine = pieces[chunk * per:(chunk + 1) * per]
        vr = jnp.concatenate([zero_rows if q is None else fv[q[0], q[1], q[2]] for q in mine], 0)
        vi = jnp.concatenate([zero_rows if q is None else fv[3 + q[0], q[1], q[2]] for q in mine], 0)
        vr = vr.T
        vi = vi.T
        lanes = slice(chunk * 128, (chunk + 1) * 128)
        lanes_i = slice(KHALF + chunk * 128, KHALF + (chunk + 1) * 128)
        for m in range(nmom):
            co = cs[0, m:m + 1, lanes]
            si = cs[1, m:m + 1, lanes]
            ar = co * vr - si * vi
            ai = -(si * vr + co * vi)
            for a, where_to in ((ar, lanes), (ai, lanes_i)):
                hi = a.astype(BF16)
                lh[m * nev:(m + 1) * nev, where_to] = hi
                ll[m * nev:(m + 1) * nev, where_to] = (a - hi.astype(F32)).astype(BF16)

    def put(row_at, half, col, value):
        hi = value.astype(BF16)
        rh[half, pl.ds(row_at, YP), col] = hi
        rl[half, pl.ds(row_at, YP), col] = (value - hi.astype(F32)).astype(BF16)

    def put_complex(row_at, half, s):
        put(row_at, half, slice(0, 128), s[0])
        put(row_at, half, slice(128, 256), s[1])
        put(row_at + KHALF, half, slice(0, 128), -s[1])
        put(row_at + KHALF, half, slice(128, 256), s[0])

    def displace(half):
        lanes = lanes_of(half)
        which = dir_ref[0:1, lanes]

        def body(x, carry):
            for z in range(LZ):
                diffs = []
                for k in range(3):
                    fwd, bwd = hops(ft, z, x, lanes, k)
                    diffs.append([(a[0] - b[0], a[1] - b[1]) for a, b in zip(fwd, bwd)])
                for c in range(3):
                    s = tuple(jnp.where(which == 0, diffs[0][c][p],
                                        jnp.where(which == 1, diffs[1][c][p], diffs[2][c][p]))
                              for p in range(2))
                    put_complex(pl.multiple_of(c * MAIN + (z * TLX + x) * YP, YP), half, s)
            return carry

        lax.fori_loop(0, TLX, body, 0)
        on_x = which == 0
        for z in range(LZ):
            high = adj(link(0, z, TLX), load(ft, z, TLX, lanes))
            low = load(ft, z, 1, lanes)
            for c in range(3):
                base = 3 * MAIN + c * HALO + z * YP
                put_complex(base, half, tuple(jnp.where(on_x, -high[c][p], 0.0) for p in range(2)))
                put_complex(base + LZ * YP, half,
                            tuple(jnp.where(on_x, low[c][p], 0.0) for p in range(2)))
        zero_tail = jnp.zeros((HALO, 256), BF16)
        for base in (KHALF - HALO, 2 * KHALF - HALO):
            rh[half, base:base + HALO, :] = zero_tail
            rl[half, base:base + HALO, :] = zero_tail

    def reversed_bits(o):
        return sum(((o >> s) & 1) << (stages - 1 - s) for s in range(stages))

    got_at = [0]
    bases = [0]
    for s in range(stages):
        got_at.append(got_at[-1] + (n >> (s + 1)))
        bases.append(bases[-1] + bits[s] * (n >> (s + 1)))
    state = {}

    def launch(job, s):
        half, m0, count = job
        size = n >> (s + 1)
        ms = pl.ds(m0, count)
        copy = pltpu.make_async_remote_copy(
            src_ref=part.at[half, ms, pl.ds(bases[s] + (1 - bits[s]) * size, size)],
            dst_ref=got.at[half, ms, pl.ds(got_at[s], size)],
            send_sem=rs_send.at[half, m0, s], recv_sem=rs_recv.at[half, m0, s],
            device_id={"site": partners[s]}, device_id_type=pl.DeviceIdType.MESH)
        copy.start()
        state[job] = (s, copy)

    def advance(job):
        s, copy = state.pop(job)
        half, m0, count = job
        copy.wait()
        size = n >> (s + 1)
        keep = pl.ds(bases[s + 1], size)
        for m in range(m0, m0 + count):
            summed = part[half, m, keep] + got[half, m, got_at[s]:got_at[s] + size]
            if s + 1 < stages:
                part[half, m, keep] = summed
            else:
                lanes = lanes_of(half)
                out_ref[:, m, 0, lanes] = summed[0, :, 0:128]
                out_ref[:, m, 1, lanes] = summed[0, :, 128:256]
        if s + 1 < stages:
            launch(job, s + 1)

    def advance_all():
        for job in list(state):
            advance(job)

    def multiply(job):
        half, m0, count = job
        take = slice(m0 * nev, (m0 + count) * nev)
        prod = jnp.dot(lh[take, :], rh[half], preferred_element_type=F32)
        prod = prod + jnp.dot(lh[take, :], rl[half], preferred_element_type=F32)
        prod = prod + jnp.dot(ll[take, :], rh[half], preferred_element_type=F32)
        for m in range(count):
            for o in range(n):
                at = m * nev + o * rows
                part[half, m0 + m, reversed_bits(o)] = prod[at:at + rows, :]

    for half in range(halves):
        receive(1, half)
        unpack(fo, 1, half)
        smear(fo, ft, half)
        advance_all()
        displace(half)
        group = 1 if half == halves - 1 else 2
        for m0 in range(0, nmom, group):
            job = (half, m0, min(group, nmom - m0))
            multiply(job)
            advance_all()
            launch(job, 0)
    while state:
        advance_all()


def site_table():
    ys = np.arange(YP)
    ys[YP - 1] = -1
    spots = [(x, y, z) for z in range(LZ) for x in range(TLX) for y in ys] * 3
    spots += [(x, y, z) for x in (TLX, -1) for z in range(LZ) for y in ys] * 4
    return np.array(spots, np.int32).T


def on_device(vectors, links, momenta, directions):
    n = lax.axis_size("site")
    tiles = math.isqrt(n)
    nev = vectors.shape[-1]
    nmom = momenta.shape[0]
    rows = nev // n
    stages = n.bit_length() - 1
    halves = nev // 128
    vmem = pl.BlockSpec(memory_space=pltpu.VMEM)
    ext = pltpu.VMEM((6, LZ, TLX + 2, YP, nev), F32)
    return pl.pallas_call(
        functools.partial(kernel, n, tiles, nmom),
        out_shape=jax.ShapeDtypeStruct((rows, nmom, 2, nev), F32),
        in_specs=[vmem] * 5,
        out_specs=vmem,
        scratch_shapes=[
            ext, ext, ext,
            pltpu.VMEM((54, LZ * (TLX + 1) * YP, 128), F32),
            pltpu.VMEM((128, 384), F32),
            pltpu.VMEM((384, 128), F32),
            pltpu.VMEM((LZ, TLX + 1, YP, 128), F32),
            pltpu.VMEM((SIDE, 128), F32),
            pltpu.VMEM((SIDE, 128), F32),
            pltpu.VMEM((2, nmom, KHALF), F32),
            pltpu.VMEM((2, halves, 4, 6, SIDE, 128), F32),
            pltpu.VMEM((2, halves, 4, 6, SIDE, 128), F32),
            pltpu.VMEM((nmom * nev, 2 * KHALF), BF16),
            pltpu.VMEM((nmom * nev, 2 * KHALF), BF16),
            pltpu.VMEM((halves, 2 * KHALF, 256), BF16),
            pltpu.VMEM((halves, 2 * KHALF, 256), BF16),
            pltpu.VMEM((halves, nmom, n, rows, 256), F32),
            pltpu.VMEM((halves, nmom, n, rows, 256), F32),
            pltpu.SemaphoreType.DMA((2, halves, 4)),
            pltpu.SemaphoreType.DMA((2, halves, 4)),
            pltpu.SemaphoreType.DMA((halves, nmom, stages)),
            pltpu.SemaphoreType.DMA((halves, nmom, stages)),
        ],
        compiler_params=pltpu.CompilerParams(
            collective_id=0, has_side_effects=True, vmem_limit_bytes=60 * 1024 * 1024),
    )(vectors, links.reshape(54, SIDE * TLY), jnp.asarray(site_table()), momenta,
      directions.reshape(1, nev))


def solution(mesh):
    placed = (
        P("grp", None, "site", None, None),
        P("grp", None, None, None, "site", None),
        P(),
        P(),
    )
    return jax.shard_map(
        on_device,
        mesh=mesh,
        in_specs=placed,
        out_specs=P("site", "grp", None, None),
        check_vma=False,
    )
```

```python
import functools
import math

import jax
import jax.numpy as jnp
import numpy as np
from jax import lax
from jax.experimental import pallas as pl
from jax.experimental.pallas import tpu as pltpu
from jax.sharding import PartitionSpec as P

TLX = 12
TLY = 12
LZ = 2
YP = 16
KAPPA = 0.08
SIDE = TLX * LZ
F32 = jnp.float32
BF16 = jnp.bfloat16
MAIN = LZ * TLX * YP
HALO = 2 * LZ * YP
KHALF = 3 * MAIN + 4 * HALO


def mat(u, f):
    out = []
    for a in range(3):
        re = im = None
        for b in range(3):
            ur, ui = u[a][b]
            fr, fi = f[b]
            tr = ur * fr - ui * fi
            ti = ur * fi + ui * fr
            re = tr if re is None else re + tr
            im = ti if im is None else im + ti
        out.append((re, im))
    return out


def adj(u, f):
    out = []
    for a in range(3):
        re = im = None
        for b in range(3):
            ur, ui = u[b][a]
            fr, fi = f[b]
            tr = ur * fr + ui * fi
            ti = ur * fi - ui * fr
            re = tr if re is None else re + tr
            im = ti if im is None else im + ti
        out.append((re, im))
    return out


def kernel(n, tiles, nmom, v_ref, lk_ref, pos_ref, mom_ref, dir_ref, out_ref,
           fv, fo, ft, ms, md, bh, bl, lkw, lkt, lkp, lkx, lky, cs, send_buf, recv_buf, lh, ll, rh, rl,
           part, got, send_sem, recv_sem, rs_send, rs_recv):
    nev = v_ref.shape[-1]
    halves = nev // 128
    rows = nev // n
    stages = n.bit_length() - 1
    me = lax.axis_index("site")
    above_x = lax.rem(me + tiles, n)
    below_x = lax.rem(me + n - tiles, n)
    above_y = lax.rem(me + 1, n)
    below_y = lax.rem(me + n - 1, n)
    partners = []
    bits = []
    for s in range(stages):
        bit = (me // (1 << s)) % 2
        bits.append(bit)
        partners.append(me + (1 - 2 * bit) * (1 << s))

    barrier = pltpu.get_barrier_semaphore()
    greeted = [above_x, below_x, above_y, below_y] + partners
    for other in greeted:
        pl.semaphore_signal(barrier, inc=1, device_id={"site": other},
                            device_id_type=pl.DeviceIdType.MESH)

    def lanes_of(half):
        return slice(half * 128, (half + 1) * 128)

    lkw[...] = jnp.zeros_like(lkw)
    lkw[0:54, 0:SIDE * TLY] = lk_ref[...]
    lkt[...] = lkw[...].T
    lane = lax.broadcasted_iota(jnp.int32, (YP, 128), 1)
    row = lax.broadcasted_iota(jnp.int32, (YP, 128), 0)
    unit_x = jnp.where((lane == 0) | (lane == 4) | (lane == 8), 1.0, 0.0)
    unit_y = jnp.where(((lane == 18) | (lane == 22) | (lane == 26)) & (row == YP - 1), 1.0, 0.0)
    for z in range(LZ):
        lkp[z, 0] = unit_x
        for x in range(TLX):
            first_row = (z * TLX + x) * TLY
            lkp[z, x + 1] = unit_y
            lkp[z, x + 1, 0:TLY, :] = lkt[first_row:first_row + TLY, :]
        last = (z + 1) * TLX * TLY - TLY
        lkx[z * TLX:(z + 1) * TLX, :] = lkt[last:last + TLY, :]
    lky[...] = lkt[pl.ds(TLY - 1, SIDE, stride=TLY), :]

    def compact(ref, k):
        def one(i):
            return jnp.broadcast_to(ref[:, 18 * k + i:18 * k + i + 1], (SIDE, 128))
        return [[(one(3 * a + b), one(9 + 3 * a + b)) for b in range(3)] for a in range(3)]

    def halo_copies(rnd, half):
        targets = (below_x, above_x, below_y, above_y)
        return [
            pltpu.make_async_remote_copy(
                src_ref=send_buf.at[rnd, half, i], dst_ref=recv_buf.at[rnd, half, i],
                send_sem=send_sem.at[rnd, half, i], recv_sem=recv_sem.at[rnd, half, i],
                device_id={"site": targets[i]}, device_id_type=pl.DeviceIdType.MESH)
            for i in range(4)
        ]

    def turn(rnd, half, slot, ref, k):
        u = compact(ref, k)
        f = [(send_buf[rnd, half, slot, b], send_buf[rnd, half, slot, 3 + b]) for b in range(3)]
        g = adj(u, f)
        for a in range(3):
            send_buf[rnd, half, slot, a] = g[a][0]
            send_buf[rnd, half, slot, 3 + a] = g[a][1]

    def pack_given(half):
        lanes = lanes_of(half)
        for c in range(6):
            p, b = c // 3, c % 3
            for z in range(LZ):
                at = z * TLX * TLY
                last = at + TLX * TLY - TLY
                to = slice(z * TLX, (z + 1) * TLX)
                send_buf[0, half, 0, c, to, :] = v_ref[p, b, 0, at:at + TLY, lanes]
                send_buf[0, half, 1, c, to, :] = v_ref[p, b, 0, last:last + TLY, lanes]
                for x in range(TLX):
                    i = z * TLX + x
                    send_buf[0, half, 2, c, i:i + 1, :] = v_ref[p, b, 0, at + x * TLY:at + x * TLY + 1, lanes]
                    y = at + x * TLY + TLY - 1
                    send_buf[0, half, 3, c, i:i + 1, :] = v_ref[p, b, 0, y:y + 1, lanes]
        turn(0, half, 1, lkx, 0)
        turn(0, half, 3, lky, 1)

    def pack(src, rnd, half):
        lanes = lanes_of(half)
        for c in range(6):
            for z in range(LZ):
                to = slice(z * TLX, (z + 1) * TLX)
                send_buf[rnd, half, 0, c, to, :] = src[c, z, 1, 0:TLY, lanes]
                send_buf[rnd, half, 1, c, to, :] = src[c, z, TLX, 0:TLY, lanes]
                send_buf[rnd, half, 2, c, to, :] = src[c, z, 1:TLX + 1, 0, lanes]
                send_buf[rnd, half, 3, c, to, :] = src[c, z, 1:TLX + 1, TLY - 1, lanes]
        turn(rnd, half, 1, lkx, 0)
        turn(rnd, half, 3, lky, 1)

    def unpack(dst, rnd, half):
        lanes = lanes_of(half)
        for c in range(6):
            for z in range(LZ):
                at = slice(z * TLX, (z + 1) * TLX)
                dst[c, z, TLX + 1, 0:TLY, lanes] = recv_buf[rnd, half, 0, c, at, :]
                dst[c, z, 0, 0:TLY, lanes] = recv_buf[rnd, half, 1, c, at, :]
                dst[c, z, 1:TLX + 1, TLY, lanes] = recv_buf[rnd, half, 2, c, at, :]
                dst[c, z, 1:TLX + 1, YP - 1, lanes] = recv_buf[rnd, half, 3, c, at, :]

    flying = {}

    def send(rnd, half):
        flying[rnd, half] = halo_copies(rnd, half)
        for copy in flying[rnd, half]:
            copy.start()

    def receive(rnd, half):
        for copy in flying[rnd, half]:
            copy.wait()

    pack_given(0)
    pl.semaphore_wait(barrier, len(greeted))
    send(0, 0)
    for half in range(1, halves):
        pack_given(half)
        send(0, half)

    zero_pad = jnp.zeros((YP - TLY, nev), F32)
    zero_rows = jnp.zeros((YP, nev), F32)
    for c in range(6):
        for z in range(LZ):
            for layer in (0, TLX + 1):
                fv[c, z, layer, TLY:YP, :] = zero_pad
                fo[c, z, layer, TLY:YP, :] = zero_pad
                ft[c, z, layer] = zero_rows
            for x in range(TLX):
                at = (z * TLX + x) * TLY
                fv[c, z, x + 1, 0:TLY, :] = v_ref[c // 3, c % 3, 0, at:at + TLY, :]
                fv[c, z, x + 1, TLY:YP, :] = zero_pad

    pad_rows = jnp.zeros((128 - 6 * YP, nev), BF16)
    for z in range(LZ):
        for layer in range(TLX + 2):
            bh[z, layer, 6 * YP:128, :] = pad_rows
            bl[z, layer, 6 * YP:128, :] = pad_rows
    segment = lane // YP
    column = lane % YP

    def masks(shift):
        return [(segment == b) & (column == (row + shift) % YP) for b in range(6)]

    same, after, before = masks(0), masks(1), masks(YP - 1)

    def spread(block, k):
        def one(i):
            return jnp.broadcast_to(block[:, 18 * k + i:18 * k + i + 1], (YP, 128))
        return [[(one(3 * a + b), one(9 + 3 * a + b)) for b in range(3)] for a in range(3)]

    def chain(where_to, coefs):
        out = jnp.zeros((YP, 128), F32)
        for b in range(6):
            out = jnp.where(where_to[b], coefs[b], out)
        return out

    def mat_row(u, cp):
        a = cp % 3
        if cp < 3:
            return [u[a][b][0] for b in range(3)] + [-u[a][b][1] for b in range(3)]
        return [u[a][b][1] for b in range(3)] + [u[a][b][0] for b in range(3)]

    def adj_row(u, cp):
        a = cp % 3
        if cp < 3:
            return [u[b][a][0] for b in range(3)] + [u[b][a][1] for b in range(3)]
        return [-u[b][a][1] for b in range(3)] + [u[b][a][0] for b in range(3)]

    def put_matrix(dst, z, x, cp, blocks):
        for j, block in enumerate(blocks):
            to = slice(j * 128, (j + 1) * 128)
            hi = block.astype(BF16)
            dst[z, x, cp * YP:(cp + 1) * YP, to] = hi
            dst[z, x, (6 + cp) * YP:(7 + cp) * YP, to] = (block - hi.astype(F32)).astype(BF16)

    def build(x, carry):
        for z in range(LZ):
            ux = spread(lkp[z, x + 1], 0)
            uxm = spread(lkp[z, x], 0)
            uy = spread(lkp[z, x + 1], 1)
            uym = spread(pltpu.roll(lkp[z, x + 1], 1, 0), 1)
            uz = spread(lkp[z, x + 1], 2)
            uzo = spread(lkp[1 - z, x + 1], 2)
            for cp in range(6):
                xb = chain(same, adj_row(uxm, cp))
                xf = chain(same, mat_row(ux, cp))
                yf = chain(after, mat_row(uy, cp))
                yb = chain(before, adj_row(uym, cp))
                zf = chain(same, mat_row(uz, cp))
                zb = chain(same, adj_row(uzo, cp))
                put_matrix(ms, z, x, cp, [xb, xf, yf + yb, zf + zb])
                put_matrix(md, z, x, cp, [-xb, xf, yf - yb, zf - zb])
        return carry

    lax.fori_loop(0, TLX, build, 0)

    lx = TLX * tiles
    ly = TLY * tiles
    gx = (me // tiles) * TLX + pos_ref[0:1, :]
    gy = (me % tiles) * TLY + pos_ref[1:2, :]
    gx = gx + jnp.where(gy >= ly, TLX, 0) - jnp.where(gy < 0, TLX, 0)
    gy = gy - jnp.where(gy >= ly, ly, 0) + jnp.where(gy < 0, ly, 0)
    gx = gx - jnp.where(gx >= lx, lx, 0) + jnp.where(gx < 0, lx, 0)
    mom = mom_ref[...].astype(F32)

    def turns(k, at, extent):
        f = mom[:, k:k + 1] * at.astype(F32) / extent
        return f - jnp.floor(f)

    theta = 2.0 * math.pi * (turns(0, gx, lx) + turns(1, gy, ly) + turns(2, pos_ref[2:3, :], LZ))
    scale = 1.0 / math.sqrt(3.0 * lx * ly * LZ)
    cs[0] = jnp.cos(theta) * scale
    cs[1] = jnp.sin(theta) * scale

    def load(src, z, layer, lanes):
        return [(src[b, z, layer, :, lanes], src[3 + b, z, layer, :, lanes]) for b in range(3)]

    def split(src, half):
        lanes = lanes_of(half)

        def body(layer, carry):
            for z in range(LZ):
                for c in range(6):
                    f = src[c, z, layer, :, lanes]
                    hi = f.astype(BF16)
                    bh[z, layer, c * YP:(c + 1) * YP, lanes] = hi
                    bl[z, layer, c * YP:(c + 1) * YP, lanes] = (f - hi.astype(F32)).astype(BF16)
            return carry

        lax.fori_loop(0, TLX + 2, body, 0)

    def near(src, z, x, lanes):
        return [src[z, x, :, lanes], src[z, x + 2, :, lanes],
                src[z, x + 1, :, lanes], src[1 - z, x + 1, :, lanes]]

    def times(matrix, z, x, cols, high, low):
        count = 6 * YP
        both = jnp.dot(matrix[z, x, :, cols], high, preferred_element_type=F32)
        rest = jnp.dot(matrix[z, x, 0:count, cols], low, preferred_element_type=F32)
        return both[0:count] + both[count:] + rest

    real_row = row < TLY

    def smear(src, dst, half):
        lanes = lanes_of(half)
        split(src, half)

        def body(x, carry):
            for z in range(LZ):
                total = times(ms, z, x, slice(0, 512), jnp.concatenate(near(bh, z, x, lanes), 0),
                              jnp.concatenate(near(bl, z, x, lanes), 0))
                for c in range(6):
                    f = src[c, z, x + 1, :, lanes]
                    new = f + KAPPA * (total[c * YP:(c + 1) * YP] - 6.0 * f)
                    dst[c, z, x + 1, :, lanes] = jnp.where(real_row, new, 0.0)
            return carry

        lax.fori_loop(0, TLX, body, 0)

    for half in range(halves):
        receive(0, half)
        unpack(fv, 0, half)
        smear(fv, fo, half)
        pack(fo, 1, half)
        send(1, half)

    pieces = []
    for c in range(3):
        pieces += [(c, z, x + 1) for z in range(LZ) for x in range(TLX)]
    for c in range(3):
        pieces += [(c, z, layer) for layer in (TLX + 1, 0) for z in range(LZ)]
    pieces += [None] * (2 * LZ)
    per = 128 // YP
    for chunk in range(KHALF // 128):
        mine = pieces[chunk * per:(chunk + 1) * per]
        vr = jnp.concatenate([zero_rows if q is None else fv[q[0], q[1], q[2]] for q in mine], 0)
        vi = jnp.concatenate([zero_rows if q is None else fv[3 + q[0], q[1], q[2]] for q in mine], 0)
        vr = vr.T
        vi = vi.T
        lanes = slice(chunk * 128, (chunk + 1) * 128)
        lanes_i = slice(KHALF + chunk * 128, KHALF + (chunk + 1) * 128)
        for m in range(nmom):
            co = cs[0, m:m + 1, lanes]
            si = cs[1, m:m + 1, lanes]
            ar = co * vr - si * vi
            ai = -(si * vr + co * vi)
            for a, where_to in ((ar, lanes), (ai, lanes_i)):
                hi = a.astype(BF16)
                lh[m * nev:(m + 1) * nev, where_to] = hi
                ll[m * nev:(m + 1) * nev, where_to] = (a - hi.astype(F32)).astype(BF16)

    def put(row_at, half, col, value):
        hi = value.astype(BF16)
        rh[half, pl.ds(row_at, YP), col] = hi
        rl[half, pl.ds(row_at, YP), col] = (value - hi.astype(F32)).astype(BF16)

    def put_complex(row_at, half, s):
        put(row_at, half, slice(0, 128), s[0])
        put(row_at, half, slice(128, 256), s[1])
        put(row_at + KHALF, half, slice(0, 128), -s[1])
        put(row_at + KHALF, half, slice(128, 256), s[0])

    def displace(half):
        lanes = lanes_of(half)
        which = dir_ref[0:1, lanes]

        split(ft, half)

        def body(x, carry):
            for z in range(LZ):
                high = near(bh, z, x, lanes)
                low = near(bl, z, x, lanes)
                diffs = []
                for cols, start, stop in ((slice(0, 256), 0, 2), (slice(256, 384), 2, 3),
                                          (slice(384, 512), 3, 4)):
                    d = times(md, z, x, cols, jnp.concatenate(high[start:stop], 0),
                              jnp.concatenate(low[start:stop], 0))
                    d = [d[c * YP:(c + 1) * YP] for c in range(6)]
                    diffs.append([(d[c], d[3 + c]) for c in range(3)])
                for c in range(3):
                    s = tuple(jnp.where(which == 0, diffs[0][c][p],
                                        jnp.where(which == 1, diffs[1][c][p], diffs[2][c][p]))
                              for p in range(2))
                    put_complex(pl.multiple_of(c * MAIN + (z * TLX + x) * YP, YP), half, s)
            return carry

        lax.fori_loop(0, TLX, body, 0)
        on_x = which == 0
        for z in range(LZ):
            high = adj(spread(lkp[z, TLX], 0), load(ft, z, TLX, lanes))
            low = load(ft, z, 1, lanes)
            for c in range(3):
                base = 3 * MAIN + c * HALO + z * YP
                put_complex(base, half, tuple(jnp.where(on_x, -high[c][p], 0.0) for p in range(2)))
                put_complex(base + LZ * YP, half,
                            tuple(jnp.where(on_x, low[c][p], 0.0) for p in range(2)))
        zero_tail = jnp.zeros((HALO, 256), BF16)
        for base in (KHALF - HALO, 2 * KHALF - HALO):
            rh[half, base:base + HALO, :] = zero_tail
            rl[half, base:base + HALO, :] = zero_tail

    def reversed_bits(o):
        return sum(((o >> s) & 1) << (stages - 1 - s) for s in range(stages))

    got_at = [0]
    bases = [0]
    for s in range(stages):
        got_at.append(got_at[-1] + (n >> (s + 1)))
        bases.append(bases[-1] + bits[s] * (n >> (s + 1)))
    state = {}

    def launch(job, s):
        half, m0, count = job
        size = n >> (s + 1)
        ms = pl.ds(m0, count)
        copy = pltpu.make_async_remote_copy(
            src_ref=part.at[half, ms, pl.ds(bases[s] + (1 - bits[s]) * size, size)],
            dst_ref=got.at[half, ms, pl.ds(got_at[s], size)],
            send_sem=rs_send.at[half, m0, s], recv_sem=rs_recv.at[half, m0, s],
            device_id={"site": partners[s]}, device_id_type=pl.DeviceIdType.MESH)
        copy.start()
        state[job] = (s, copy)

    def advance(job):
        s, copy = state.pop(job)
        half, m0, count = job
        copy.wait()
        size = n >> (s + 1)
        keep = pl.ds(bases[s + 1], size)
        for m in range(m0, m0 + count):
            summed = part[half, m, keep] + got[half, m, got_at[s]:got_at[s] + size]
            if s + 1 < stages:
                part[half, m, keep] = summed
            else:
                lanes = lanes_of(half)
                out_ref[:, m, 0, lanes] = summed[0, :, 0:128]
                out_ref[:, m, 1, lanes] = summed[0, :, 128:256]
        if s + 1 < stages:
            launch(job, s + 1)

    def advance_all():
        for job in list(state):
            advance(job)

    def multiply(job):
        half, m0, count = job
        take = slice(m0 * nev, (m0 + count) * nev)
        prod = jnp.dot(lh[take, :], rh[half], preferred_element_type=F32)
        prod = prod + jnp.dot(lh[take, :], rl[half], preferred_element_type=F32)
        prod = prod + jnp.dot(ll[take, :], rh[half], preferred_element_type=F32)
        for m in range(count):
            for o in range(n):
                at = m * nev + o * rows
                part[half, m0 + m, reversed_bits(o)] = prod[at:at + rows, :]

    for half in range(halves):
        receive(1, half)
        unpack(fo, 1, half)
        smear(fo, ft, half)
        advance_all()
        displace(half)
        group = 1 if half == halves - 1 else 2
        for m0 in range(0, nmom, group):
            job = (half, m0, min(group, nmom - m0))
            multiply(job)
            advance_all()
            launch(job, 0)
    while state:
        advance_all()


def site_table():
    ys = np.arange(YP)
    ys[YP - 1] = -1
    spots = [(x, y, z) for z in range(LZ) for x in range(TLX) for y in ys] * 3
    spots += [(x, y, z) for x in (TLX, -1) for z in range(LZ) for y in ys] * 4
    return np.array(spots, np.int32).T


def on_device(vectors, links, momenta, directions):
    n = lax.axis_size("site")
    tiles = math.isqrt(n)
    nev = vectors.shape[-1]
    nmom = momenta.shape[0]
    rows = nev // n
    stages = n.bit_length() - 1
    halves = nev // 128
    vmem = pl.BlockSpec(memory_space=pltpu.VMEM)
    ext = pltpu.VMEM((6, LZ, TLX + 2, YP, nev), F32)
    return pl.pallas_call(
        functools.partial(kernel, n, tiles, nmom),
        out_shape=jax.ShapeDtypeStruct((rows, nmom, 2, nev), F32),
        in_specs=[vmem] * 5,
        out_specs=vmem,
        scratch_shapes=[
            ext, ext, ext,
            pltpu.VMEM((LZ, TLX, 12 * YP, 512), BF16),
            pltpu.VMEM((LZ, TLX, 12 * YP, 512), BF16),
            pltpu.VMEM((LZ, TLX + 2, 128, nev), BF16),
            pltpu.VMEM((LZ, TLX + 2, 128, nev), BF16),
            pltpu.VMEM((128, 384), F32),
            pltpu.VMEM((384, 128), F32),
            pltpu.VMEM((LZ, TLX + 1, YP, 128), F32),
            pltpu.VMEM((SIDE, 128), F32),
            pltpu.VMEM((SIDE, 128), F32),
            pltpu.VMEM((2, nmom, KHALF), F32),
            pltpu.VMEM((2, halves, 4, 6, SIDE, 128), F32),
            pltpu.VMEM((2, halves, 4, 6, SIDE, 128), F32),
            pltpu.VMEM((nmom * nev, 2 * KHALF), BF16),
            pltpu.VMEM((nmom * nev, 2 * KHALF), BF16),
            pltpu.VMEM((halves, 2 * KHALF, 256), BF16),
            pltpu.VMEM((halves, 2 * KHALF, 256), BF16),
            pltpu.VMEM((halves, nmom, n, rows, 256), F32),
            pltpu.VMEM((halves, nmom, n, rows, 256), F32),
            pltpu.SemaphoreType.DMA((2, halves, 4)),
            pltpu.SemaphoreType.DMA((2, halves, 4)),
            pltpu.SemaphoreType.DMA((halves, nmom, stages)),
            pltpu.SemaphoreType.DMA((halves, nmom, stages)),
        ],
        compiler_params=pltpu.CompilerParams(
            collective_id=0, has_side_effects=True, vmem_limit_bytes=60 * 1024 * 1024),
    )(vectors, links.reshape(54, SIDE * TLY), jnp.asarray(site_table()), momenta,
      directions.reshape(1, nev))


def solution(mesh):
    placed = (
        P("grp", None, "site", None, None),
        P("grp", None, None, None, "site", None),
        P(),
        P(),
    )
    return jax.shard_map(
        on_device,
        mesh=mesh,
        in_specs=placed,
        out_specs=P("site", "grp", None, None),
        check_vma=False,
    )
```

```python
import functools
import math

import jax
import jax.numpy as jnp
import numpy as np
from jax import lax
from jax.experimental import pallas as pl
from jax.experimental.pallas import tpu as pltpu
from jax.sharding import PartitionSpec as P

TLX = 12
TLY = 12
LZ = 2
YP = 16
KAPPA = 0.08
SIDE = TLX * LZ
F32 = jnp.float32
BF16 = jnp.bfloat16
MAIN = LZ * TLX * YP
HALO = 2 * LZ * YP
KHALF = 3 * MAIN + 4 * HALO


def mat(u, f):
    out = []
    for a in range(3):
        re = im = None
        for b in range(3):
            ur, ui = u[a][b]
            fr, fi = f[b]
            tr = ur * fr - ui * fi
            ti = ur * fi + ui * fr
            re = tr if re is None else re + tr
            im = ti if im is None else im + ti
        out.append((re, im))
    return out


def adj(u, f):
    out = []
    for a in range(3):
        re = im = None
        for b in range(3):
            ur, ui = u[b][a]
            fr, fi = f[b]
            tr = ur * fr + ui * fi
            ti = ur * fi - ui * fr
            re = tr if re is None else re + tr
            im = ti if im is None else im + ti
        out.append((re, im))
    return out


def kernel(n, tiles, nmom, v_ref, lk_ref, pos_ref, mom_ref, dir_ref, out_ref,
           fv, fo, ft, links, lkw, lkt, lkp, lkx, lky, cs, turned, flat, send_buf, recv_buf, lh, ll, rh, rl,
           part, got, send_sem, recv_sem, rs_send, rs_recv):
    nev = v_ref.shape[-1]
    halves = nev // 128
    rows = nev // n
    stages = n.bit_length() - 1
    me = lax.axis_index("site")
    above_x = lax.rem(me + tiles, n)
    below_x = lax.rem(me + n - tiles, n)
    above_y = lax.rem(me + 1, n)
    below_y = lax.rem(me + n - 1, n)
    partners = []
    bits = []
    for s in range(stages):
        bit = (me // (1 << s)) % 2
        bits.append(bit)
        partners.append(me + (1 - 2 * bit) * (1 << s))

    barrier = pltpu.get_barrier_semaphore()
    greeted = [above_x, below_x, above_y, below_y] + partners
    for other in greeted:
        pl.semaphore_signal(barrier, inc=1, device_id={"site": other},
                            device_id_type=pl.DeviceIdType.MESH)

    def lanes_of(half):
        return slice(half * 128, (half + 1) * 128)

    lkw[...] = jnp.zeros_like(lkw)
    lkw[0:54, 0:SIDE * TLY] = lk_ref[...]
    lkt[...] = lkw[...].T
    lane = lax.broadcasted_iota(jnp.int32, (YP, 128), 1)
    row = lax.broadcasted_iota(jnp.int32, (YP, 128), 0)
    unit_x = jnp.where((lane == 0) | (lane == 4) | (lane == 8), 1.0, 0.0)
    unit_y = jnp.where(((lane == 18) | (lane == 22) | (lane == 26)) & (row == YP - 1), 1.0, 0.0)
    for z in range(LZ):
        lkp[z, 0] = unit_x
        for x in range(TLX):
            first_row = (z * TLX + x) * TLY
            lkp[z, x + 1] = unit_y
            lkp[z, x + 1, 0:TLY, :] = lkt[first_row:first_row + TLY, :]
        last = (z + 1) * TLX * TLY - TLY
        lkx[z * TLX:(z + 1) * TLX, :] = lkt[last:last + TLY, :]
    lky[...] = lkt[pl.ds(TLY - 1, SIDE, stride=TLY), :]

    def compact(ref, k):
        def one(i):
            return jnp.broadcast_to(ref[:, 18 * k + i:18 * k + i + 1], (SIDE, 128))
        return [[(one(3 * a + b), one(9 + 3 * a + b)) for b in range(3)] for a in range(3)]

    def halo_copies(rnd, half):
        targets = (below_x, above_x, below_y, above_y)
        return [
            pltpu.make_async_remote_copy(
                src_ref=send_buf.at[rnd, half, i], dst_ref=recv_buf.at[rnd, half, i],
                send_sem=send_sem.at[rnd, half, i], recv_sem=recv_sem.at[rnd, half, i],
                device_id={"site": targets[i]}, device_id_type=pl.DeviceIdType.MESH)
            for i in range(4)
        ]

    def turn(rnd, half, slot, ref, k):
        u = compact(ref, k)
        f = [(send_buf[rnd, half, slot, b], send_buf[rnd, half, slot, 3 + b]) for b in range(3)]
        g = adj(u, f)
        for a in range(3):
            send_buf[rnd, half, slot, a] = g[a][0]
            send_buf[rnd, half, slot, 3 + a] = g[a][1]

    def each(count, body):
        def step(i, carry):
            body(i)
            return carry
        lax.fori_loop(0, count, step, 0)

    def pack_given(half):
        lanes = lanes_of(half)

        def one(c):
            p, b = c // 3, c % 3
            for z in range(LZ):
                at = z * TLX * TLY
                last = at + TLX * TLY - TLY
                to = slice(z * TLX, (z + 1) * TLX)
                send_buf[0, half, 0, c, to, :] = v_ref[p, b, 0, at:at + TLY, lanes]
                send_buf[0, half, 1, c, to, :] = v_ref[p, b, 0, last:last + TLY, lanes]
                for x in range(TLX):
                    i = z * TLX + x
                    send_buf[0, half, 2, c, i:i + 1, :] = v_ref[p, b, 0, at + x * TLY:at + x * TLY + 1, lanes]
                    y = at + x * TLY + TLY - 1
                    send_buf[0, half, 3, c, i:i + 1, :] = v_ref[p, b, 0, y:y + 1, lanes]

        each(6, one)
        turn(0, half, 1, lkx, 0)
        turn(0, half, 3, lky, 1)

    def pack(src, rnd, half):
        lanes = lanes_of(half)

        def one(c):
            for z in range(LZ):
                to = slice(z * TLX, (z + 1) * TLX)
                send_buf[rnd, half, 0, c, to, :] = src[c, z, 1, 0:TLY, lanes]
                send_buf[rnd, half, 1, c, to, :] = src[c, z, TLX, 0:TLY, lanes]
                send_buf[rnd, half, 2, c, to, :] = src[c, z, 1:TLX + 1, 0, lanes]
                send_buf[rnd, half, 3, c, to, :] = src[c, z, 1:TLX + 1, TLY - 1, lanes]

        each(6, one)
        turn(rnd, half, 1, lkx, 0)
        turn(rnd, half, 3, lky, 1)

    def unpack(dst, rnd, half):
        lanes = lanes_of(half)

        def one(c):
            for z in range(LZ):
                at = slice(z * TLX, (z + 1) * TLX)
                dst[c, z, TLX + 1, 0:TLY, lanes] = recv_buf[rnd, half, 0, c, at, :]
                dst[c, z, 0, 0:TLY, lanes] = recv_buf[rnd, half, 1, c, at, :]
                dst[c, z, 1:TLX + 1, TLY, lanes] = recv_buf[rnd, half, 2, c, at, :]
                dst[c, z, 1:TLX + 1, YP - 1, lanes] = recv_buf[rnd, half, 3, c, at, :]

        each(6, one)

    flying = {}

    def send(rnd, half):
        flying[rnd, half] = halo_copies(rnd, half)
        for copy in flying[rnd, half]:
            copy.start()

    def receive(rnd, half):
        for copy in flying[rnd, half]:
            copy.wait()

    pack_given(0)
    pl.semaphore_wait(barrier, len(greeted))
    send(0, 0)
    for half in range(1, halves):
        pack_given(half)
        send(0, half)

    zero_pad = jnp.zeros((YP - TLY, nev), F32)
    zero_rows = jnp.zeros((YP, nev), F32)
    def own(c):
        for z in range(LZ):
            for layer in (0, TLX + 1):
                fv[c, z, layer, TLY:YP, :] = zero_pad
                ft[c, z, layer] = zero_rows
            for x in range(TLX):
                at = (z * TLX + x) * TLY
                fv[c, z, x + 1, 0:TLY, :] = v_ref[c // 3, c % 3, 0, at:at + TLY, :]
                fv[c, z, x + 1, TLY:YP, :] = zero_pad

    each(6, own)

    def spread(r, carry):
        at = pl.multiple_of(r * YP, YP)
        block = lkp[r // (TLX + 1), r % (TLX + 1)]
        for k in range(54):
            links[k, pl.ds(at, YP), :] = jnp.broadcast_to(block[:, k:k + 1], (YP, 128))
        return carry

    lax.fori_loop(0, LZ * (TLX + 1), spread, 0)

    lx = TLX * tiles
    ly = TLY * tiles
    gx = (me // tiles) * TLX + pos_ref[0:1, :]
    gy = (me % tiles) * TLY + pos_ref[1:2, :]
    gx = gx + jnp.where(gy >= ly, TLX, 0) - jnp.where(gy < 0, TLX, 0)
    gy = gy - jnp.where(gy >= ly, ly, 0) + jnp.where(gy < 0, ly, 0)
    gx = gx - jnp.where(gx >= lx, lx, 0) + jnp.where(gx < 0, lx, 0)
    mom = mom_ref[...].astype(F32)

    def turns(k, at, extent):
        f = mom[:, k:k + 1] * at.astype(F32) / extent
        return f - jnp.floor(f)

    theta = 2.0 * math.pi * (turns(0, gx, lx) + turns(1, gy, ly) + turns(2, pos_ref[2:3, :], LZ))
    scale = 1.0 / math.sqrt(3.0 * lx * ly * LZ)
    cosine = jnp.cos(theta) * scale
    sine = jnp.sin(theta) * scale
    for m in range(nmom):
        cs[0, m] = cosine[m:m + 1, :]
        cs[1, m] = sine[m:m + 1, :]

    def link(k, z, layer):
        at = pl.multiple_of((z * (TLX + 1) + layer) * YP, YP)
        def one(i):
            return links[18 * k + i, pl.ds(at, YP), :]
        return [[(one(3 * a + b), one(9 + 3 * a + b)) for b in range(3)] for a in range(3)]

    def load(src, z, layer, lanes):
        return [(src[b, z, layer, :, lanes], src[3 + b, z, layer, :, lanes]) for b in range(3)]

    def roll(f, shift):
        return [(pltpu.roll(r, shift, 0), pltpu.roll(i, shift, 0)) for r, i in f]

    def hops(src, z, x, lanes, k):
        f = load(src, z, x + 1, lanes)
        if k == 0:
            return (mat(link(0, z, x + 1), load(src, z, x + 2, lanes)),
                    adj(link(0, z, x), load(src, z, x, lanes)))
        if k == 1:
            u = link(1, z, x + 1)
            return mat(u, roll(f, YP - 1)), roll(adj(u, f), 1)
        other = load(src, 1 - z, x + 1, lanes)
        return mat(link(2, z, x + 1), other), adj(link(2, 1 - z, x + 1), other)

    real_row = row < TLY

    def smear(src, dst, half):
        lanes = lanes_of(half)

        def body(x, carry):
            for z in range(LZ):
                total = None
                for k in range(3):
                    fwd, bwd = hops(src, z, x, lanes, k)
                    term = [(a[0] + b[0], a[1] + b[1]) for a, b in zip(fwd, bwd)]
                    total = term if total is None else [
                        (a[0] + b[0], a[1] + b[1]) for a, b in zip(total, term)]
                f = load(src, z, x + 1, lanes)
                for a in range(3):
                    for p in range(2):
                        new = f[a][p] + KAPPA * (total[a][p] - 6.0 * f[a][p])
                        dst[3 * p + a, z, x + 1, :, lanes] = jnp.where(real_row, new, 0.0)
            return carry

        lax.fori_loop(0, TLX, body, 0)

    for half in range(halves):
        receive(0, half)
        unpack(fv, 0, half)
        smear(fv, fo, half)
        pack(fo, 1, half)
        send(1, half)

    def left_chunk(at, where):
        for i in range(128 // YP):
            c, z, layer = where(i)
            turned[0, i * YP:(i + 1) * YP, :] = fv[c, z, layer]
            turned[1, i * YP:(i + 1) * YP, :] = fv[3 + c, z, layer]
        vr = turned[0].T
        vi = turned[1].T
        lanes = pl.ds(pl.multiple_of(at, 128), 128)
        lanes_i = pl.ds(pl.multiple_of(KHALF + at, 128), 128)
        flat[0] = vr
        flat[1] = vi

        def one(m):
            rows_m = pl.ds(pl.multiple_of(m * nev, nev), nev)
            co = cs[0, m, :, lanes]
            si = cs[1, m, :, lanes]
            re = flat[0]
            im = flat[1]
            for a, where_to in ((co * re - si * im, lanes), (-(si * re + co * im), lanes_i)):
                hi = a.astype(BF16)
                lh[rows_m, where_to] = hi
                ll[rows_m, where_to] = (a - hi.astype(F32)).astype(BF16)

        each(nmom, one)

    per = 128 // YP

    def main_chunk(q):
        def where(i):
            at = (q % 3) * per + i
            return q // 3, at // TLX, at % TLX + 1
        left_chunk(q * 128, where)

    def halo_chunk(q):
        def where(i):
            at = q * per + i
            return jnp.minimum(at // (2 * LZ), 2), at % LZ, (TLX + 1) * (1 - (at // LZ) % 2)
        left_chunk(3 * MAIN + q * 128, where)

    each(3 * MAIN // 128, main_chunk)
    each(4 * HALO // 128, halo_chunk)

    def put(row_at, half, col, value):
        hi = value.astype(BF16)
        rh[half, pl.ds(row_at, YP), col] = hi
        rl[half, pl.ds(row_at, YP), col] = (value - hi.astype(F32)).astype(BF16)

    def put_complex(row_at, half, s):
        put(row_at, half, slice(0, 128), s[0])
        put(row_at, half, slice(128, 256), s[1])
        put(row_at + KHALF, half, slice(0, 128), -s[1])
        put(row_at + KHALF, half, slice(128, 256), s[0])

    def displace(half):
        lanes = lanes_of(half)
        which = dir_ref[0:1, lanes]

        def body(x, carry):
            for z in range(LZ):
                diffs = []
                for k in range(3):
                    fwd, bwd = hops(ft, z, x, lanes, k)
                    diffs.append([(a[0] - b[0], a[1] - b[1]) for a, b in zip(fwd, bwd)])
                for c in range(3):
                    s = tuple(jnp.where(which == 0, diffs[0][c][p],
                                        jnp.where(which == 1, diffs[1][c][p], diffs[2][c][p]))
                              for p in range(2))
                    put_complex(pl.multiple_of(c * MAIN + (z * TLX + x) * YP, YP), half, s)
            return carry

        lax.fori_loop(0, TLX, body, 0)
        on_x = which == 0
        for z in range(LZ):
            high = adj(link(0, z, TLX), load(ft, z, TLX, lanes))
            low = load(ft, z, 1, lanes)
            for c in range(3):
                base = 3 * MAIN + c * HALO + z * YP
                put_complex(base, half, tuple(jnp.where(on_x, -high[c][p], 0.0) for p in range(2)))
                put_complex(base + LZ * YP, half,
                            tuple(jnp.where(on_x, low[c][p], 0.0) for p in range(2)))
        zero_tail = jnp.zeros((HALO, 256), BF16)
        for base in (KHALF - HALO, 2 * KHALF - HALO):
            rh[half, base:base + HALO, :] = zero_tail
            rl[half, base:base + HALO, :] = zero_tail

    def reversed_bits(o):
        return sum(((o >> s) & 1) << (stages - 1 - s) for s in range(stages))

    got_at = [0]
    bases = [0]
    for s in range(stages):
        got_at.append(got_at[-1] + (n >> (s + 1)))
        bases.append(bases[-1] + bits[s] * (n >> (s + 1)))
    state = {}

    def launch(job, s):
        half, m0, count = job
        size = n >> (s + 1)
        ms = pl.ds(m0, count)
        copy = pltpu.make_async_remote_copy(
            src_ref=part.at[half, ms, pl.ds(bases[s] + (1 - bits[s]) * size, size)],
            dst_ref=got.at[half, ms, pl.ds(got_at[s], size)],
            send_sem=rs_send.at[half, m0, s], recv_sem=rs_recv.at[half, m0, s],
            device_id={"site": partners[s]}, device_id_type=pl.DeviceIdType.MESH)
        copy.start()
        state[job] = (s, copy)

    def advance(job):
        s, copy = state.pop(job)
        half, m0, count = job
        copy.wait()
        size = n >> (s + 1)
        keep = pl.ds(bases[s + 1], size)
        for m in range(m0, m0 + count):
            if s + 1 == stages:
                summed = part[half, m, keep] + got[half, m, got_at[s]:got_at[s] + size]
                lanes = lanes_of(half)
                out_ref[:, m, 0, lanes] = summed[0, :, 0:128]
                out_ref[:, m, 1, lanes] = summed[0, :, 128:256]
        if s + 1 < stages:
            def add(i):
                m = m0 + i // size
                o = i % size
                at = bases[s + 1] + o
                part[half, m, at] = part[half, m, at] + got[half, m, got_at[s] + o]
            each(count * size, add)
        if s + 1 < stages:
            launch(job, s + 1)

    def advance_all():
        for job in list(state):
            advance(job)

    def multiply(job):
        half, m0, count = job

        def one(i):
            m = m0 + i
            take = pl.ds(pl.multiple_of(m * nev, nev), nev)
            prod = jnp.dot(lh[take, :], rh[half], preferred_element_type=F32)
            prod = prod + jnp.dot(lh[take, :], rl[half], preferred_element_type=F32)
            prod = prod + jnp.dot(ll[take, :], rh[half], preferred_element_type=F32)
            for o in range(n):
                part[half, m, reversed_bits(o)] = prod[o * rows:(o + 1) * rows, :]

        each(count, one)

    for half in range(halves):
        receive(1, half)
        unpack(fo, 1, half)
        smear(fo, ft, half)
        advance_all()
        displace(half)
        group = 2 if half == halves - 1 else nmom
        for m0 in range(0, nmom, group):
            job = (half, m0, min(group, nmom - m0))
            multiply(job)
            advance_all()
            launch(job, 0)
    while state:
        advance_all()


def site_table():
    ys = np.arange(YP)
    ys[YP - 1] = -1
    spots = [(x, y, z) for z in range(LZ) for x in range(TLX) for y in ys] * 3
    spots += [(x, y, z) for x in (TLX, -1) for z in range(LZ) for y in ys] * 4
    return np.array(spots, np.int32).T


def on_device(vectors, links, momenta, directions):
    n = lax.axis_size("site")
    tiles = math.isqrt(n)
    nev = vectors.shape[-1]
    nmom = momenta.shape[0]
    rows = nev // n
    stages = n.bit_length() - 1
    halves = nev // 128
    vmem = pl.BlockSpec(memory_space=pltpu.VMEM)
    ext = pltpu.VMEM((6, LZ, TLX + 2, YP, nev), F32)
    return pl.pallas_call(
        functools.partial(kernel, n, tiles, nmom),
        out_shape=jax.ShapeDtypeStruct((rows, nmom, 2, nev), F32),
        in_specs=[vmem] * 5,
        out_specs=vmem,
        scratch_shapes=[
            ext, ext, ext,
            pltpu.VMEM((54, LZ * (TLX + 1) * YP, 128), F32),
            pltpu.VMEM((128, 384), F32),
            pltpu.VMEM((384, 128), F32),
            pltpu.VMEM((LZ, TLX + 1, YP, 128), F32),
            pltpu.VMEM((SIDE, 128), F32),
            pltpu.VMEM((SIDE, 128), F32),
            pltpu.VMEM((2, nmom, 1, KHALF), F32),
            pltpu.VMEM((2, 128, nev), F32),
            pltpu.VMEM((2, nev, 128), F32),
            pltpu.VMEM((2, halves, 4, 6, SIDE, 128), F32),
            pltpu.VMEM((2, halves, 4, 6, SIDE, 128), F32),
            pltpu.VMEM((nmom * nev, 2 * KHALF), BF16),
            pltpu.VMEM((nmom * nev, 2 * KHALF), BF16),
            pltpu.VMEM((halves, 2 * KHALF, 256), BF16),
            pltpu.VMEM((halves, 2 * KHALF, 256), BF16),
            pltpu.VMEM((halves, nmom, n, rows, 256), F32),
            pltpu.VMEM((halves, nmom, n, rows, 256), F32),
            pltpu.SemaphoreType.DMA((2, halves, 4)),
            pltpu.SemaphoreType.DMA((2, halves, 4)),
            pltpu.SemaphoreType.DMA((halves, nmom, stages)),
            pltpu.SemaphoreType.DMA((halves, nmom, stages)),
        ],
        compiler_params=pltpu.CompilerParams(
            collective_id=0, has_side_effects=True, vmem_limit_bytes=60 * 1024 * 1024),
    )(vectors, links.reshape(54, SIDE * TLY), jnp.asarray(site_table()), momenta,
      directions.reshape(1, nev))


def solution(mesh):
    placed = (
        P("grp", None, "site", None, None),
        P("grp", None, None, None, "site", None),
        P(),
        P(),
    )
    return jax.shard_map(
        on_device,
        mesh=mesh,
        in_specs=placed,
        out_specs=P("site", "grp", None, None),
        check_vma=False,
    )
```

```python
import functools
import math

import jax
import jax.numpy as jnp
import numpy as np
from jax import lax
from jax.experimental import pallas as pl
from jax.experimental.pallas import tpu as pltpu
from jax.sharding import PartitionSpec as P

TLX = 12
TLY = 12
LZ = 2
YP = 16
KAPPA = 0.08
SIDE = TLX * LZ
F32 = jnp.float32
BF16 = jnp.bfloat16
MAIN = LZ * TLX * YP
HALO = 2 * LZ * YP
KHALF = 3 * MAIN + 4 * HALO


def mat(u, f):
    out = []
    for a in range(3):
        re = im = None
        for b in range(3):
            ur, ui = u[a][b]
            fr, fi = f[b]
            tr = ur * fr - ui * fi
            ti = ur * fi + ui * fr
            re = tr if re is None else re + tr
            im = ti if im is None else im + ti
        out.append((re, im))
    return out


def adj(u, f):
    out = []
    for a in range(3):
        re = im = None
        for b in range(3):
            ur, ui = u[b][a]
            fr, fi = f[b]
            tr = ur * fr + ui * fi
            ti = ur * fi - ui * fr
            re = tr if re is None else re + tr
            im = ti if im is None else im + ti
        out.append((re, im))
    return out


def kernel(n, tiles, nmom, v_ref, lk_ref, pos_ref, mom_ref, dir_ref, out_ref,
           fv, fo, ft, links, lkw, lkt, lkp, lkx, lky, cs, turned, flat, send_buf, recv_buf, lh, ll, rh, rl,
           part, got, send_sem, recv_sem, rs_send, rs_recv):
    nev = v_ref.shape[-1]
    halves = nev // 128
    rows = nev // n
    stages = n.bit_length() - 1
    me = lax.axis_index("site")
    above_x = lax.rem(me + tiles, n)
    below_x = lax.rem(me + n - tiles, n)
    above_y = lax.rem(me + 1, n)
    below_y = lax.rem(me + n - 1, n)
    partners = []
    bits = []
    for s in range(stages):
        bit = (me // (1 << s)) % 2
        bits.append(bit)
        partners.append(me + (1 - 2 * bit) * (1 << s))

    barrier = pltpu.get_barrier_semaphore()
    greeted = [above_x, below_x, above_y, below_y] + partners
    for other in greeted:
        pl.semaphore_signal(barrier, inc=1, device_id={"site": other},
                            device_id_type=pl.DeviceIdType.MESH)

    def lanes_of(half):
        return slice(half * 128, (half + 1) * 128)

    lkw[...] = jnp.zeros_like(lkw)
    for i in range(54):
        k, p, a, b = i // 18, i // 9 % 2, i // 3 % 3, i % 3
        lkw[i:i + 1, 0:SIDE * TLY] = lk_ref[k, p, a, b]
    lkt[...] = lkw[...].T
    lane = lax.broadcasted_iota(jnp.int32, (YP, 128), 1)
    row = lax.broadcasted_iota(jnp.int32, (YP, 128), 0)
    unit_x = jnp.where((lane == 0) | (lane == 4) | (lane == 8), 1.0, 0.0)
    unit_y = jnp.where(((lane == 18) | (lane == 22) | (lane == 26)) & (row == YP - 1), 1.0, 0.0)
    for z in range(LZ):
        lkp[z, 0] = unit_x
        for x in range(TLX):
            first_row = (z * TLX + x) * TLY
            lkp[z, x + 1] = unit_y
            lkp[z, x + 1, 0:TLY, :] = lkt[first_row:first_row + TLY, :]
        last = (z + 1) * TLX * TLY - TLY
        lkx[z * TLX:(z + 1) * TLX, :] = lkt[last:last + TLY, :]
    lky[...] = lkt[pl.ds(TLY - 1, SIDE, stride=TLY), :]

    def compact(ref, k):
        def one(i):
            return jnp.broadcast_to(ref[:, 18 * k + i:18 * k + i + 1], (SIDE, 128))
        return [[(one(3 * a + b), one(9 + 3 * a + b)) for b in range(3)] for a in range(3)]

    def halo_copies(rnd, half):
        targets = (below_x, above_x, below_y, above_y)
        return [
            pltpu.make_async_remote_copy(
                src_ref=send_buf.at[rnd, half, i], dst_ref=recv_buf.at[rnd, half, i],
                send_sem=send_sem.at[rnd, half, i], recv_sem=recv_sem.at[rnd, half, i],
                device_id={"site": targets[i]}, device_id_type=pl.DeviceIdType.MESH)
            for i in range(4)
        ]

    def turn(rnd, half, slot, ref, k):
        u = compact(ref, k)
        f = [(send_buf[rnd, half, slot, b], send_buf[rnd, half, slot, 3 + b]) for b in range(3)]
        g = adj(u, f)
        for a in range(3):
            send_buf[rnd, half, slot, a] = g[a][0]
            send_buf[rnd, half, slot, 3 + a] = g[a][1]

    def each(count, body):
        def step(i, carry):
            body(i)
            return carry
        lax.fori_loop(0, count, step, 0)

    def pack_given(half):
        lanes = lanes_of(half)

        def one(c):
            p, b = c // 3, c % 3
            for z in range(LZ):
                at = z * TLX * TLY
                last = at + TLX * TLY - TLY
                to = slice(z * TLX, (z + 1) * TLX)
                send_buf[0, half, 0, c, to, :] = v_ref[p, b, 0, at:at + TLY, lanes]
                send_buf[0, half, 1, c, to, :] = v_ref[p, b, 0, last:last + TLY, lanes]
                for x in range(TLX):
                    i = z * TLX + x
                    send_buf[0, half, 2, c, i:i + 1, :] = v_ref[p, b, 0, at + x * TLY:at + x * TLY + 1, lanes]
                    y = at + x * TLY + TLY - 1
                    send_buf[0, half, 3, c, i:i + 1, :] = v_ref[p, b, 0, y:y + 1, lanes]

        each(6, one)
        turn(0, half, 1, lkx, 0)
        turn(0, half, 3, lky, 1)

    def pack(src, rnd, half):
        lanes = lanes_of(half)

        def one(c):
            for z in range(LZ):
                to = slice(z * TLX, (z + 1) * TLX)
                send_buf[rnd, half, 0, c, to, :] = src[c, z, 1, 0:TLY, lanes]
                send_buf[rnd, half, 1, c, to, :] = src[c, z, TLX, 0:TLY, lanes]
                send_buf[rnd, half, 2, c, to, :] = src[c, z, 1:TLX + 1, 0, lanes]
                send_buf[rnd, half, 3, c, to, :] = src[c, z, 1:TLX + 1, TLY - 1, lanes]

        each(6, one)
        turn(rnd, half, 1, lkx, 0)
        turn(rnd, half, 3, lky, 1)

    def unpack(dst, rnd, half):
        lanes = lanes_of(half)

        def one(c):
            for z in range(LZ):
                at = slice(z * TLX, (z + 1) * TLX)
                dst[c, z, TLX + 1, 0:TLY, lanes] = recv_buf[rnd, half, 0, c, at, :]
                dst[c, z, 0, 0:TLY, lanes] = recv_buf[rnd, half, 1, c, at, :]
                dst[c, z, 1:TLX + 1, TLY, lanes] = recv_buf[rnd, half, 2, c, at, :]
                dst[c, z, 1:TLX + 1, YP - 1, lanes] = recv_buf[rnd, half, 3, c, at, :]

        each(6, one)

    flying = {}

    def send(rnd, half):
        flying[rnd, half] = halo_copies(rnd, half)
        for copy in flying[rnd, half]:
            copy.start()

    def receive(rnd, half):
        for copy in flying[rnd, half]:
            copy.wait()

    pack_given(0)
    pl.semaphore_wait(barrier, len(greeted))
    send(0, 0)
    for half in range(1, halves):
        pack_given(half)
        send(0, half)

    zero_pad = jnp.zeros((YP - TLY, nev), F32)
    zero_rows = jnp.zeros((YP, nev), F32)
    def own(c):
        for z in range(LZ):
            for layer in (0, TLX + 1):
                fv[c, z, layer, TLY:YP, :] = zero_pad
                ft[c, z, layer] = zero_rows
            for x in range(TLX):
                at = (z * TLX + x) * TLY
                fv[c, z, x + 1, 0:TLY, :] = v_ref[c // 3, c % 3, 0, at:at + TLY, :]
                fv[c, z, x + 1, TLY:YP, :] = zero_pad

    each(6, own)

    def spread(r, carry):
        at = pl.multiple_of(r * YP, YP)
        block = lkp[r // (TLX + 1), r % (TLX + 1)]
        for k in range(54):
            links[k, pl.ds(at, YP), :] = jnp.broadcast_to(block[:, k:k + 1], (YP, 128))
        return carry

    lax.fori_loop(0, LZ * (TLX + 1), spread, 0)

    lx = TLX * tiles
    ly = TLY * tiles
    gx = (me // tiles) * TLX + pos_ref[0:1, :]
    gy = (me % tiles) * TLY + pos_ref[1:2, :]
    gx = gx + jnp.where(gy >= ly, TLX, 0) - jnp.where(gy < 0, TLX, 0)
    gy = gy - jnp.where(gy >= ly, ly, 0) + jnp.where(gy < 0, ly, 0)
    gx = gx - jnp.where(gx >= lx, lx, 0) + jnp.where(gx < 0, lx, 0)
    mom = mom_ref[...].astype(F32)

    def turns(k, at, extent):
        f = mom[:, k:k + 1] * at.astype(F32) / extent
        return f - jnp.floor(f)

    theta = 2.0 * math.pi * (turns(0, gx, lx) + turns(1, gy, ly) + turns(2, pos_ref[2:3, :], LZ))
    scale = 1.0 / math.sqrt(3.0 * lx * ly * LZ)
    cosine = jnp.cos(theta) * scale
    sine = jnp.sin(theta) * scale
    for m in range(nmom):
        cs[0, m] = cosine[m:m + 1, :]
        cs[1, m] = sine[m:m + 1, :]

    def link(k, z, layer):
        at = pl.multiple_of((z * (TLX + 1) + layer) * YP, YP)
        def one(i):
            return links[18 * k + i, pl.ds(at, YP), :]
        return [[(one(3 * a + b), one(9 + 3 * a + b)) for b in range(3)] for a in range(3)]

    def load(src, z, layer, lanes):
        return [(src[b, z, layer, :, lanes], src[3 + b, z, layer, :, lanes]) for b in range(3)]

    def roll(f, shift):
        return [(pltpu.roll(r, shift, 0), pltpu.roll(i, shift, 0)) for r, i in f]

    def hops(src, z, x, lanes, k):
        f = load(src, z, x + 1, lanes)
        if k == 0:
            return (mat(link(0, z, x + 1), load(src, z, x + 2, lanes)),
                    adj(link(0, z, x), load(src, z, x, lanes)))
        if k == 1:
            u = link(1, z, x + 1)
            return mat(u, roll(f, YP - 1)), roll(adj(u, f), 1)
        other = load(src, 1 - z, x + 1, lanes)
        return mat(link(2, z, x + 1), other), adj(link(2, 1 - z, x + 1), other)

    real_row = row < TLY

    def smear(src, dst, half):
        lanes = lanes_of(half)

        def body(x, carry):
            for z in range(LZ):
                total = None
                for k in range(3):
                    fwd, bwd = hops(src, z, x, lanes, k)
                    term = [(a[0] + b[0], a[1] + b[1]) for a, b in zip(fwd, bwd)]
                    total = term if total is None else [
                        (a[0] + b[0], a[1] + b[1]) for a, b in zip(total, term)]
                f = load(src, z, x + 1, lanes)
                for a in range(3):
                    for p in range(2):
                        new = f[a][p] + KAPPA * (total[a][p] - 6.0 * f[a][p])
                        dst[3 * p + a, z, x + 1, :, lanes] = jnp.where(real_row, new, 0.0)
            return carry

        lax.fori_loop(0, TLX, body, 0)

    for half in range(halves):
        receive(0, half)
        unpack(fv, 0, half)
        smear(fv, fo, half)
        pack(fo, 1, half)
        send(1, half)

    def left_chunk(at, where):
        for i in range(128 // YP):
            c, z, layer = where(i)
            turned[0, i * YP:(i + 1) * YP, :] = fv[c, z, layer]
            turned[1, i * YP:(i + 1) * YP, :] = fv[3 + c, z, layer]
        vr = turned[0].T
        vi = turned[1].T
        lanes = pl.ds(pl.multiple_of(at, 128), 128)
        lanes_i = pl.ds(pl.multiple_of(KHALF + at, 128), 128)
        flat[0] = vr
        flat[1] = vi

        def one(m):
            rows_m = pl.ds(pl.multiple_of(m * nev, nev), nev)
            co = cs[0, m, :, lanes]
            si = cs[1, m, :, lanes]
            re = flat[0]
            im = flat[1]
            for a, where_to in ((co * re - si * im, lanes), (-(si * re + co * im), lanes_i)):
                hi = a.astype(BF16)
                lh[rows_m, where_to] = hi
                ll[rows_m, where_to] = (a - hi.astype(F32)).astype(BF16)

        each(nmom, one)

    per = 128 // YP

    def main_chunk(q):
        def where(i):
            at = (q % 3) * per + i
            return q // 3, at // TLX, at % TLX + 1
        left_chunk(q * 128, where)

    def halo_chunk(q):
        def where(i):
            at = q * per + i
            return jnp.minimum(at // (2 * LZ), 2), at % LZ, (TLX + 1) * (1 - (at // LZ) % 2)
        left_chunk(3 * MAIN + q * 128, where)

    each(3 * MAIN // 128, main_chunk)
    each(4 * HALO // 128, halo_chunk)

    def put(row_at, half, col, value):
        hi = value.astype(BF16)
        rh[half, pl.ds(row_at, YP), col] = hi
        rl[half, pl.ds(row_at, YP), col] = (value - hi.astype(F32)).astype(BF16)

    def put_complex(row_at, half, s):
        put(row_at, half, slice(0, 128), s[0])
        put(row_at, half, slice(128, 256), s[1])
        put(row_at + KHALF, half, slice(0, 128), -s[1])
        put(row_at + KHALF, half, slice(128, 256), s[0])

    def displace(half):
        lanes = lanes_of(half)
        which = dir_ref[0:1, lanes]

        def body(x, carry):
            for z in range(LZ):
                diffs = []
                for k in range(3):
                    fwd, bwd = hops(ft, z, x, lanes, k)
                    diffs.append([(a[0] - b[0], a[1] - b[1]) for a, b in zip(fwd, bwd)])
                for c in range(3):
                    s = tuple(jnp.where(which == 0, diffs[0][c][p],
                                        jnp.where(which == 1, diffs[1][c][p], diffs[2][c][p]))
                              for p in range(2))
                    put_complex(pl.multiple_of(c * MAIN + (z * TLX + x) * YP, YP), half, s)
            return carry

        lax.fori_loop(0, TLX, body, 0)
        on_x = which == 0
        for z in range(LZ):
            high = adj(link(0, z, TLX), load(ft, z, TLX, lanes))
            low = load(ft, z, 1, lanes)
            for c in range(3):
                base = 3 * MAIN + c * HALO + z * YP
                put_complex(base, half, tuple(jnp.where(on_x, -high[c][p], 0.0) for p in range(2)))
                put_complex(base + LZ * YP, half,
                            tuple(jnp.where(on_x, low[c][p], 0.0) for p in range(2)))
        zero_tail = jnp.zeros((HALO, 256), BF16)
        for base in (KHALF - HALO, 2 * KHALF - HALO):
            rh[half, base:base + HALO, :] = zero_tail
            rl[half, base:base + HALO, :] = zero_tail

    def reversed_bits(o):
        return sum(((o >> s) & 1) << (stages - 1 - s) for s in range(stages))

    got_at = [0]
    bases = [0]
    for s in range(stages):
        got_at.append(got_at[-1] + (n >> (s + 1)))
        bases.append(bases[-1] + bits[s] * (n >> (s + 1)))
    state = {}

    def launch(job, s):
        half, m0, count = job
        size = n >> (s + 1)
        ms = pl.ds(m0, count)
        copy = pltpu.make_async_remote_copy(
            src_ref=part.at[half, ms, pl.ds(bases[s] + (1 - bits[s]) * size, size)],
            dst_ref=got.at[half, ms, pl.ds(got_at[s], size)],
            send_sem=rs_send.at[half, m0, s], recv_sem=rs_recv.at[half, m0, s],
            device_id={"site": partners[s]}, device_id_type=pl.DeviceIdType.MESH)
        copy.start()
        state[job] = (s, copy)

    def advance(job):
        s, copy = state.pop(job)
        half, m0, count = job
        copy.wait()
        size = n >> (s + 1)
        keep = pl.ds(bases[s + 1], size)
        for m in range(m0, m0 + count):
            if s + 1 == stages:
                summed = part[half, m, keep] + got[half, m, got_at[s]:got_at[s] + size]
                lanes = lanes_of(half)
                out_ref[:, 2 * m, lanes] = summed[0, :, 0:128]
                out_ref[:, 2 * m + 1, lanes] = summed[0, :, 128:256]
        if s + 1 < stages:
            def add(i):
                m = m0 + i // size
                o = i % size
                at = bases[s + 1] + o
                part[half, m, at] = part[half, m, at] + got[half, m, got_at[s] + o]
            each(count * size, add)
        if s + 1 < stages:
            launch(job, s + 1)

    def advance_all():
        for job in list(state):
            advance(job)

    def multiply(job):
        half, m0, count = job

        def one(i):
            m = m0 + i
            take = pl.ds(pl.multiple_of(m * nev, nev), nev)
            prod = jnp.dot(lh[take, :], rh[half], preferred_element_type=F32)
            prod = prod + jnp.dot(lh[take, :], rl[half], preferred_element_type=F32)
            prod = prod + jnp.dot(ll[take, :], rh[half], preferred_element_type=F32)
            for o in range(n):
                part[half, m, reversed_bits(o)] = prod[o * rows:(o + 1) * rows, :]

        each(count, one)

    for half in range(halves):
        receive(1, half)
        unpack(fo, 1, half)
        smear(fo, ft, half)
        advance_all()
        displace(half)
        group = 2 if half == halves - 1 else nmom
        for m0 in range(0, nmom, group):
            job = (half, m0, min(group, nmom - m0))
            multiply(job)
            advance_all()
            launch(job, 0)
    while state:
        advance_all()


def site_table():
    ys = np.arange(YP)
    ys[YP - 1] = -1
    spots = [(x, y, z) for z in range(LZ) for x in range(TLX) for y in ys] * 3
    spots += [(x, y, z) for x in (TLX, -1) for z in range(LZ) for y in ys] * 4
    return np.array(spots, np.int32).T


def on_device(vectors, links, momenta, directions):
    n = lax.axis_size("site")
    tiles = math.isqrt(n)
    nev = vectors.shape[-1]
    nmom = momenta.shape[0]
    rows = nev // n
    stages = n.bit_length() - 1
    halves = nev // 128
    vmem = pl.BlockSpec(memory_space=pltpu.VMEM)
    ext = pltpu.VMEM((6, LZ, TLX + 2, YP, nev), F32)
    out = pl.pallas_call(
        functools.partial(kernel, n, tiles, nmom),
        out_shape=jax.ShapeDtypeStruct((rows, 2 * nmom, nev), F32),
        in_specs=[vmem] * 5,
        out_specs=vmem,
        scratch_shapes=[
            ext, ext, ext,
            pltpu.VMEM((54, LZ * (TLX + 1) * YP, 128), F32),
            pltpu.VMEM((128, 384), F32),
            pltpu.VMEM((384, 128), F32),
            pltpu.VMEM((LZ, TLX + 1, YP, 128), F32),
            pltpu.VMEM((SIDE, 128), F32),
            pltpu.VMEM((SIDE, 128), F32),
            pltpu.VMEM((2, nmom, 1, KHALF), F32),
            pltpu.VMEM((2, 128, nev), F32),
            pltpu.VMEM((2, nev, 128), F32),
            pltpu.VMEM((2, halves, 4, 6, SIDE, 128), F32),
            pltpu.VMEM((2, halves, 4, 6, SIDE, 128), F32),
            pltpu.VMEM((nmom * nev, 2 * KHALF), BF16),
            pltpu.VMEM((nmom * nev, 2 * KHALF), BF16),
            pltpu.VMEM((halves, 2 * KHALF, 256), BF16),
            pltpu.VMEM((halves, 2 * KHALF, 256), BF16),
            pltpu.VMEM((halves, nmom, n, rows, 256), F32),
            pltpu.VMEM((halves, nmom, n, rows, 256), F32),
            pltpu.SemaphoreType.DMA((2, halves, 4)),
            pltpu.SemaphoreType.DMA((2, halves, 4)),
            pltpu.SemaphoreType.DMA((halves, nmom, stages)),
            pltpu.SemaphoreType.DMA((halves, nmom, stages)),
        ],
        compiler_params=pltpu.CompilerParams(
            collective_id=0, has_side_effects=True, vmem_limit_bytes=60 * 1024 * 1024),
    )(vectors, links, jnp.asarray(site_table()), momenta,
      directions.reshape(1, nev))
    return out.reshape(rows, nmom, 2, nev)


def solution(mesh):
    placed = (
        P("grp", None, "site", None, None),
        P("grp", None, None, None, "site", None),
        P(),
        P(),
    )
    return jax.shard_map(
        on_device,
        mesh=mesh,
        in_specs=placed,
        out_specs=P("site", "grp", None, None),
        check_vma=False,
    )
```
